128 devices in a mesh: index: 32 (over z, y, core), rep: 4 (over x).
Axes of the slice: x: 4, y: 4, z: 4, core: 2. Of those that a mesh axis runs over, the one named last changes fastest.
Arguments:
- queries: bfloat16 [1536, 32, 128], P('index'), may hold values from -32 to 32
- listed: int32 [1536, 8], P('index'), may hold values from 0 to 2047, as said below
- page_slot: int32 [2048], replicated, may hold values from 0 to 2047, as said below
- counts: int32 [2048], P('index'), may hold values from 768 to 1024
- page_store: bfloat16 [2048, 1024, 128], P('index', 'rep'), may hold values from -18 to 18
Outputs:
- losses: float32 [1536], P('index')
- query_grads: bfloat16 [1536, 32, 128], P('index')
The draws below stay inside these ranges and needn't reach their ends.
Inputs may be any that keep to these rules, and one draw needn't show every extreme that they name: Page ids; the 8 pages of a query are different. Storage row r lies on index r // 64. Over the 48 queries of one index, at most 24 listed pages lie on any one index, and in every draw one index is named exactly 24 times by the queries of every index. The k-th page of a query lies at row (o + k) mod 64 of its index, for one offset o per query. `page_slot`: A permutation of the page ids.
All inputs are finite; a program needn't handle non-finite values.
Results may differ from the reference program's by a relative error of at most 0.01785.
Values may be sent and summed in bfloat16 or wider, within the bound.
No kernel may reach another device: no remote copies, remote signals or barrier semaphores. Data moves between devices by JAX's collectives and lax.ppermute only.
A program may use at most 128 MiB of HBM per device.

```python
import math
import jax
import jax.numpy as jnp
from jax import lax

W = 128
QT = 32
LISTED = 8
PATCHES = 1024
PAGES_DEV = 64
QDEV = 48
NQ = 1536
NP = 2048
N_INDEX = 32
N_REP = 4


def route_tables(key):
    base_key = jax.random.fold_in(key, 100)
    total_pages = PAGES_DEV * N_INDEX
    page_slot = jax.random.permutation(jax.random.fold_in(base_key, 0), total_pages).astype(jnp.int32)
    inverse = jnp.zeros((total_pages,), jnp.int32).at[page_slot].set(jnp.arange(total_pages, dtype=jnp.int32))
    capacity = 2 * QDEV * LISTED // N_INDEX
    pair_count = QDEV * LISTED
    hot_owner = jax.random.randint(jax.random.fold_in(base_key, 1), (), 0, N_INDEX).astype(jnp.int32)
    pool = ((hot_owner + 1 + jnp.arange((N_INDEX - 1) * capacity, dtype=jnp.int32) // capacity) % N_INDEX).astype(jnp.int32)

    def one_source(source):
        source_key = jax.random.fold_in(base_key, 1000 + source)
        taken = jax.random.permutation(jax.random.fold_in(source_key, 0), pool)[:pair_count - capacity]
        owners = jnp.concatenate([jnp.full((capacity,), hot_owner, jnp.int32), taken])
        owners = jax.random.permutation(jax.random.fold_in(source_key, 1), owners)
        offset = jax.random.randint(jax.random.fold_in(source_key, 2), (QDEV, 1), 0, PAGES_DEV).astype(jnp.int32)
        local_rows = (offset + jnp.arange(LISTED, dtype=jnp.int32)[None, :]) % PAGES_DEV
        stored = owners.reshape(QDEV, LISTED) * PAGES_DEV + local_rows
        return inverse[stored]
    listed = jax.vmap(one_source)(jnp.arange(N_INDEX, dtype=jnp.int32)).reshape(QDEV * N_INDEX, LISTED)
    return (page_slot, listed.astype(jnp.int32))


def page_key(key, stored_row):
    return jax.random.fold_in(jax.random.fold_in(key, 200), stored_row)


def row_scales(key, count, low, high):
    return jnp.exp(jax.random.uniform(key, (count, 1), jnp.float32, math.log(low), math.log(high)))


def head_rows(key, stored_row, low, high):
    base_key = page_key(key, stored_row)
    first = jnp.clip(jax.random.normal(jax.random.fold_in(base_key, 0), (2, W), jnp.float32), -6.0, 6.0)
    second = first[1]
    rows = jnp.stack([first[0], second])
    return rows * row_scales(jax.random.fold_in(base_key, 2), 2, low, high)


def tail_rows(key, stored_row, low, high):
    base_key = page_key(key, stored_row)
    rest = jnp.clip(jax.random.normal(jax.random.fold_in(base_key, 1), (PATCHES - 2, W), jnp.float32), -6.0, 6.0)
    return rest * row_scales(jax.random.fold_in(base_key, 3), PATCHES - 2, low, high)


def draw_page_slot(key, part):
    page_slot, listed = route_tables(key)
    return page_slot


def draw_listed(key, part):
    page_slot, listed = route_tables(key)
    return listed


def draw_page_store(key, part):
    low, high, head_low, head_high = (0.5, 2.0, 0.5, 2.0)

    def one_page(stored_row):
        return jnp.concatenate([head_rows(key, stored_row, head_low, head_high), tail_rows(key, stored_row, low, high)], axis=0)
    pages = lax.map(one_page, jnp.arange(PAGES_DEV * N_INDEX, dtype=jnp.int32))
    return jnp.clip(pages, -18.0, 18.0).astype(jnp.bfloat16)


def draw_queries(key, part):
    page_slot, listed = route_tables(key)
    head_low, head_high, jitter_top = (0.5, 2.0, 0.0)
    query_total = QDEV * N_INDEX
    aligned_count = min(QT, LISTED)
    stored = page_slot[listed[:, :aligned_count]].reshape(query_total * aligned_count)

    def drawn_row(stored_row):
        return head_rows(key, stored_row, head_low, head_high)[0]
    heads = lax.map(drawn_row, stored)
    own_key = jax.random.fold_in(key, 7)
    base = jnp.clip(jax.random.normal(jax.random.fold_in(own_key, 0), (query_total, QT, W), jnp.float32), -6.0, 6.0) * 0.1
    jitter_draw = jax.random.uniform(jax.random.fold_in(own_key, 3), (query_total, aligned_count), jnp.float32, 0.0, 1.0)
    strength = jitter_top * jitter_draw
    strength = strength.reshape(query_total * aligned_count, 1)
    norms = jnp.sum(heads * heads, axis=1, keepdims=True)
    aligned = (strength * math.sqrt(W) / norms * heads).reshape(query_total, aligned_count, W)
    base = base.at[:, :aligned_count, :].add(aligned)
    return jnp.clip(base, -32.0, 32.0).astype(jnp.bfloat16)


def set_ends(array, key, low, high):
    extent = array.shape
    index_at = [jax.random.randint(jax.random.fold_in(key, axis), (), 0, extent[axis]) for axis in range(len(extent))]
    array = array.at[tuple(index_at)].set(low)
    longest = extent.index(max(extent))
    index_at[longest] = (index_at[longest] + 1) % extent[longest]
    return array.at[tuple(index_at)].set(high)


def setup_inputs(seed: int = 0) -> dict:
    key_list = jax.random.split(jax.random.key(seed), 6)
    queries = draw_queries(jax.random.fold_in(key_list[5], 71), 0)
    listed = draw_listed(jax.random.fold_in(key_list[5], 71), 0)
    page_slot = draw_page_slot(jax.random.fold_in(key_list[5], 71), 0)
    counts = set_ends(jax.random.randint(key_list[3], (NP,), 3 * PATCHES // 4, PATCHES + 1), jax.random.fold_in(key_list[3], 1), 3 * PATCHES // 4, PATCHES).astype(jnp.int32)
    page_store = draw_page_store(jax.random.fold_in(key_list[5], 71), 0)
    return dict(queries=queries, listed=listed, page_slot=page_slot, counts=counts, page_store=page_store)


TAU = 0.1
LOSS_SCALE = 32.0
NEG = -1e+30

def query_block(tokens, page_rows, counts, page_store):
    batch = page_rows.shape[0]
    page_data = page_store[page_rows].astype(jnp.float32)
    page_data = page_data.reshape(batch, LISTED, N_REP, PATCHES // N_REP, W)
    limits = counts[page_rows]
    position = jnp.arange(PATCHES, dtype=jnp.int32).reshape(N_REP, PATCHES // N_REP)
    usable = position[None, None, :, None, :] < limits[:, :, None, None, None]
    sim_scale = 1.0 / (math.sqrt(W) * TAU)
    logits = jnp.einsum('btw,bkhpw->bkhtp', tokens.astype(jnp.float32), page_data) * sim_scale
    logits = jnp.where(usable, logits, NEG)
    peaks = lax.optimization_barrier(jnp.max(logits, axis=4))
    weights = jnp.where(usable, jnp.exp(logits - peaks[..., None]), 0.0)
    totals = lax.optimization_barrier(jnp.sum(weights, axis=4))
    rounded = lax.optimization_barrier(weights.astype(jnp.bfloat16)).astype(jnp.float32)
    vectors = jnp.einsum('bkhtp,bkhpw->bkhtw', rounded, page_data)
    largest = lax.optimization_barrier(jnp.max(peaks, axis=2))
    shares = jnp.exp(peaks - largest[:, :, None, :])
    denominator = lax.optimization_barrier(jnp.sum(totals * shares, axis=2))
    scaled_parts = lax.optimization_barrier((vectors * shares[..., None]).astype(jnp.bfloat16)).astype(jnp.float32)
    summed = lax.optimization_barrier(jnp.sum(scaled_parts, axis=2))
    scores = lax.optimization_barrier(jnp.sum(TAU * (largest + jnp.log(denominator)), axis=2))
    directions = lax.optimization_barrier((summed / (denominator[..., None] * math.sqrt(W))).astype(jnp.bfloat16)).astype(jnp.float32)
    highest = lax.optimization_barrier(jnp.max(scores, axis=1, keepdims=True))
    log_total = highest[:, 0] + jnp.log(lax.optimization_barrier(jnp.sum(jnp.exp(scores - highest), axis=1)))
    losses = log_total - scores[:, 0]
    probability = jnp.exp(scores - log_total[:, None])
    target = (jnp.arange(LISTED) == 0).astype(jnp.float32)
    coefficient = LOSS_SCALE * (probability - target[None, :])
    gradients = lax.optimization_barrier(jnp.sum(coefficient[:, :, None, None] * directions, axis=1)).astype(jnp.bfloat16)
    return (losses, gradients)

def reference(queries, listed, page_slot, counts, page_store):
    page_rows = page_slot[listed]
    block_count = NQ // 8

    def one_block(inputs):
        return query_block(inputs[0], inputs[1], counts, page_store)
    losses, gradients = lax.map(one_block, (queries.reshape(block_count, 8, QT, W), page_rows.reshape(block_count, 8, LISTED)))
    return (losses.reshape(NQ), gradients.reshape(NQ, QT, W))
```

```python
import functools
import math

import jax
import jax.numpy as jnp
from jax import lax
from jax.experimental import pallas as pl
from jax.experimental.pallas import tpu as pltpu
from jax.sharding import PartitionSpec as P

TAU = 0.1
LOSS_SCALE = 32.0
NEG = -1e30
BLOCK = 4
UNROLL = 4
RING = 4
F32 = jnp.float32
BF16 = jnp.bfloat16

SMEM = pl.BlockSpec(memory_space=pltpu.SMEM)
VMEM = pl.BlockSpec(memory_space=pltpu.VMEM)
ANY = pl.BlockSpec(memory_space=pl.ANY)


def params(mib):
    return pltpu.CompilerParams(vmem_limit_bytes=mib * 1024 * 1024)


def place_of(z, y, core):
    return ((z % RING) * RING + (y % RING)) * 2 + core


def ring_pairs(second, step):
    pairs = []
    for z in range(RING):
        for y in range(RING):
            for core in range(2):
                if (core == 0) != second:
                    there = place_of(z, y + step, core)
                else:
                    there = place_of(z + step, y, core)
                pairs.append((place_of(z, y, core), there))
    return pairs


CORE_PAIRS = [(i, i ^ 1) for i in range(2 * RING * RING)]


def across(x):
    return lax.ppermute(x, "index", CORE_PAIRS)


def gather_queries(queries, core):
    half = queries.shape[0] // 2
    keep = lax.dynamic_slice_in_dim(queries, core * half, half, 0)
    give = lax.dynamic_slice_in_dim(queries, (1 - core) * half, half, 0)
    got = across(give)
    own = jnp.where(core == 0, jnp.stack([keep, got]), jnp.stack([got, keep]))

    def spread(x, second):
        n = x.shape[0] // 2
        right = lax.ppermute(x, "index", ring_pairs(second, 1))
        left = lax.ppermute(x, "index", ring_pairs(second, -1))
        far_a = lax.ppermute(right[:n], "index", ring_pairs(second, 1))
        far_b = lax.ppermute(left[n:], "index", ring_pairs(second, -1))
        return right, left, far_a, far_b

    right, left, far_a, far_b = spread(own, False)
    own_spread = spread(own, True)
    rest = jnp.concatenate([right, left, far_a, far_b], axis=0)
    rest_spread = spread(rest, True)
    pieces = []
    for p, x in enumerate((own, own_spread[0], own_spread[1])):
        pieces.append((x, 8 * p))
    pieces.append((own_spread[2], 24))
    pieces.append((own_spread[3], 25))
    for p, x in enumerate((rest, rest_spread[0], rest_spread[1])):
        pieces.append((x, 8 * p + 2))
    pieces.append((rest_spread[2], 26))
    pieces.append((rest_spread[3], 29))
    swapped = [(across(x), 32 + at) for x, at in pieces]
    return pieces + swapped


def route_kernel(capacity, pages, list_len, listed, page_slot, table, place, used):
    slots = table.shape[0]
    pairs = listed.shape[0]

    def clear(i, _):
        for k in range(8):
            table[i * 8 + k] = -1
        return 0

    lax.fori_loop(0, slots // 8, clear, 0)

    def clear_used(i, _):
        used[i] = 0
        return 0

    lax.fori_loop(0, used.shape[0], clear_used, 0)

    def step(q, _):
        for k in range(list_len):
            i = q * list_len + k
            row = page_slot[listed[i]]
            owner = row // pages
            n = used[owner]
            used[owner] = n + 1
            j = owner * capacity + jnp.minimum(n, capacity - 1)
            table[j] = q * pages + (row - owner * pages)
            place[i] = j
        return 0

    lax.fori_loop(0, pairs // list_len, step, 0)


def sort_kernel(
    capacity, pages, half, blocks, arrived, me, order, slot_pad, slot_at, block_page, block_at, block_count, count, start, first
):
    slots = arrived.shape[0]
    groups = slots // capacity
    z = me[0] // (2 * RING)
    y = (me[0] // 2) % RING
    core = me[0] % 2

    def clear(i, _):
        for k in range(8):
            order[i * 8 + k] = 0
            slot_pad[i * 8 + k] = -1
        return 0

    lax.fori_loop(0, blocks * BLOCK // 8, clear, 0)

    def clear_blocks(i, _):
        block_page[i] = 0
        block_at[i] = slots
        return 0

    lax.fori_loop(0, blocks, clear_blocks, 0)

    def clear_count(i, _):
        count[i] = 0
        return 0

    lax.fori_loop(0, pages + 1, clear_count, 0)

    def bucket(code):
        return jnp.where(code < 0, pages, code % pages)

    def tally(i, _):
        for k in range(8):
            p = bucket(arrived[i * 8 + k])
            count[p] = count[p] + 1
        return 0

    lax.fori_loop(0, slots // 8, tally, 0)

    def lay(p, carry):
        at, b = carry
        n = count[p]
        start[p] = at
        first[p] = b * BLOCK
        count[p] = 0
        steps = (n + BLOCK - 1) // BLOCK

        def one(k, _):
            block_page[b + k] = p
            block_at[b + k] = at + k * BLOCK
            return 0

        lax.fori_loop(0, steps, one, 0)
        return at + n, b + steps

    at, total = lax.fori_loop(0, pages, lay, (jnp.int32(0), jnp.int32(0)))
    block_count[0] = total
    start[pages] = at
    first[pages] = blocks * BLOCK
    count[pages] = 0

    def rank(there, mine):
        apart = (there - mine + RING) % RING
        return jnp.where(apart == 0, 0, jnp.where(apart == RING - 1, 1, jnp.where(apart == 1, 2, 3)))

    def source(s, _):
        dz = rank(s // (2 * RING), z)
        dy = rank((s // 2) % RING, y)
        sc = s % 2
        low = ((jnp.where(core == 0, 0, RING) + dz) * RING + dy) * 2 + sc
        high = ((jnp.where(core == 1, 0, RING) + dy) * RING + dz) * 2 + sc
        low_base = low * half
        high_base = high * half - half

        def inner(j, _):
            i = s * capacity + j
            code = arrived[i]
            p = bucket(code)
            q = jnp.maximum(code, 0) // pages
            r = count[p]
            count[p] = r + 1
            e = first[p] + r
            order[e] = q + jnp.where(q < half, low_base, high_base)
            slot_pad[e] = i
            slot_at[start[p] + r] = i
            return 0

        lax.fori_loop(0, capacity, inner, 0)
        return 0

    lax.fori_loop(0, groups, source, 0)


def pair_kernel(places, scale, order, block_page, block_at, block_count, limits, *refs):
    n_pieces = len(places)
    store = refs[0]
    pieces = refs[1 : 1 + n_pieces]
    vectors, peaks, totals, held, pages, sems = refs[1 + n_pieces :]
    copies = [pltpu.make_async_copy(store, pages, sems.at[n_pieces])]
    for k, (ref, at) in enumerate(zip(pieces, places, strict=True)):
        copies.append(pltpu.make_async_copy(ref, held.at[pl.ds(at, ref.shape[0])], sems.at[k]))
    for c in copies:
        c.start()
    for c in copies:
        c.wait()
    part = pages.shape[1]
    rows = BLOCK * held.shape[1]
    feature = held.shape[2]
    power = scale * math.log2(math.e)
    lane = lax.broadcasted_iota(jnp.int32, (1, part), 1)
    eye = lax.broadcasted_iota(jnp.int32, (rows, rows), 0) == lax.broadcasted_iota(jnp.int32, (rows, rows), 1)

    def as_row(column):
        return jnp.sum(jnp.where(eye, column, 0.0), axis=0, keepdims=True)

    def step(it, _):
        for u in range(UNROLL):
            b = it * UNROLL + u
            p = block_page[b]
            tokens = jnp.concatenate([held[order[b * BLOCK + i]] for i in range(BLOCK)], axis=0)
            page = pages[p]
            raw = lax.dot_general(tokens, page, (((1,), (1,)), ((), ())), preferred_element_type=F32)
            raw = jnp.where(lane < limits[p], raw, NEG)
            top = jnp.max(raw, axis=1, keepdims=True)
            weights = jnp.exp2((raw - top) * power)
            total = jnp.sum(weights, axis=1, keepdims=True)
            out = jnp.dot(weights.astype(BF16), page, preferred_element_type=F32)
            vectors[pl.ds(block_at[b], BLOCK)] = out.astype(BF16).reshape(BLOCK, rows // BLOCK, feature)
            peaks[pl.ds(b, 1), :] = as_row(jnp.maximum(top * scale, NEG))
            totals[pl.ds(b, 1), :] = as_row(total)
        return 0

    lax.fori_loop(0, (block_count[0] + UNROLL - 1) // UNROLL, step, 0)


def scale_kernel(root, block_at, block_count, me, slot_cols, *refs):
    stats = refs[:8]
    vectors = refs[8]
    outs = refs[9:17]
    scores = refs[17]
    factors, logs, wide = refs[18:]
    peaks, totals = stats[:4], stats[4:]
    blocks, rows = factors.shape
    tokens = rows // BLOCK
    feature = vectors.shape[2]
    largest = functools.reduce(jnp.maximum, [p[...] for p in peaks])
    shares = [jnp.exp(p[...] - largest) for p in peaks]
    denominator = sum(t[...] * s for t, s in zip(totals, shares, strict=True))
    factors[...] = shares[0] / (denominator * root)
    logs[...] = TAU * (largest + jnp.log(denominator))

    lanes = lax.broadcasted_iota(jnp.int32, (8, 128), 1)
    n_rows = scores.shape[0]

    def score(v, acc):
        at = pl.multiple_of(v * 8, 8)
        block = logs[pl.ds(at, 8), :]
        cols = slot_cols[pl.ds(at, 8), :]
        acc = list(acc)
        for i in range(BLOCK):
            value = jnp.sum(jnp.where(lanes // tokens == i, block, 0.0), axis=1, keepdims=True)
            slot = cols[:, i : i + 1]
            for k in range(n_rows):
                acc[k] = jnp.where(lanes + 128 * k == slot, value, acc[k])
        return tuple(acc)

    acc = lax.fori_loop(0, blocks // 8, score, tuple(jnp.zeros((8, 128), F32) for _ in range(n_rows)))
    scores[...] = jnp.concatenate([jnp.sum(a, axis=0, keepdims=True) for a in acc], axis=0)

    eye = lax.broadcasted_iota(jnp.int32, (rows, rows), 0) == lax.broadcasted_iota(jnp.int32, (rows, rows), 1)
    share = tokens // 4

    def step(it, _):
        for u in range(UNROLL):
            b = it * UNROLL + u
            row = factors[pl.ds(b, 1), :]
            column = jnp.sum(jnp.where(eye, row, 0.0), axis=1, keepdims=True)
            at = block_at[b]
            block = vectors[pl.ds(at, BLOCK)].astype(F32).reshape(rows, feature) * column
            for i in range(BLOCK):
                for t in range(4):
                    first = i * tokens + t * share
                    wide[t, pl.ds(pl.multiple_of((at + i) * share, share), share), :] = block[first : first + share]
        return 0

    lax.fori_loop(0, (block_count[0] + UNROLL - 1) // UNROLL, step, 0)

    rep = me[1]
    length = outs[0].shape[0]
    chunk = 128
    for p in range(4):
        t = (rep + p) % 4
        for h in range(2):

            def narrow(i, _):
                at = pl.multiple_of(i * chunk, chunk)
                outs[p * 2 + h][pl.ds(at, chunk), :] = wide[t, pl.ds(at + h * length, chunk), :].astype(BF16)
                return 0

            lax.fori_loop(0, length // chunk, narrow, 0)


def slot_kernel(share, slot_at, in_a, own_a, in_b, own_b, out, wide):
    chunk = 16
    for h, (x, own) in enumerate(((in_a, own_a), (in_b, own_b))):
        length = x.shape[0]
        per = chunk // share

        def move(i, _):
            for k in range(4):
                at = pl.multiple_of((i * 4 + k) * chunk, chunk)
                both = x[pl.ds(at, chunk), :].astype(F32) + own[pl.ds(at, chunk), :].astype(F32)
                for s in range(per):
                    slot = slot_at[h * (length // share) + (i * 4 + k) * per + s]
                    wide[pl.ds(pl.multiple_of(slot * share, share), share), :] = both[s * share : (s + 1) * share]
            return 0

        lax.fori_loop(0, length // chunk // 4, move, 0)

    def narrow(i, _):
        at = pl.multiple_of(i * 128, 128)
        out[pl.ds(at, 128), :] = wide[pl.ds(at, 128), :].astype(BF16)
        return 0

    lax.fori_loop(0, out.shape[0] // 128, narrow, 0)


def gradient_kernel(share, list_len, place, weight, directions, out, wide):
    def widen(i, _):
        at = pl.multiple_of(i * 128, 128)
        wide[pl.ds(at, 128), :] = directions[pl.ds(at, 128), :].astype(F32)
        return 0

    lax.fori_loop(0, directions.shape[0] // 128, widen, 0)

    def step(i, _):
        parts = []
        for s in range(2):
            total = jnp.zeros((share, out.shape[1]), F32)
            for k in range(list_len):
                e = (i * 2 + s) * list_len + k
                at = pl.multiple_of(place[e] * share, share)
                total = total + weight[e] * wide[pl.ds(at, share), :]
            parts.append(total)
        out[pl.ds(pl.multiple_of(i * 2 * share, 2 * share), 2 * share), :] = jnp.concatenate(parts, axis=0).astype(BF16)
        return 0

    lax.fori_loop(0, out.shape[0] // share // 2, step, 0)


def ints(*shape):
    return jax.ShapeDtypeStruct(shape, jnp.int32)


def per_device(queries, listed, page_slot, counts, page_store):
    groups = lax.axis_size("index")
    index = lax.axis_index("index").astype(jnp.int32)
    rep = lax.axis_index("rep").astype(jnp.int32)
    reps = lax.axis_size("rep")
    query_count, query_len, feature = queries.shape
    list_len = listed.shape[1]
    pages, part, _ = page_store.shape
    pairs = query_count * list_len
    capacity = 2 * pairs // groups
    slots = groups * capacity
    half = query_count // 2
    share = query_len // reps
    blocks = (slots + (BLOCK - 1) * pages) // BLOCK
    blocks = (blocks + 7) // 8 * 8
    rows = BLOCK * query_len
    me = jnp.stack([index, rep])

    table, place = pl.pallas_call(
        functools.partial(route_kernel, capacity, pages, list_len),
        out_shape=(ints(slots), ints(pairs)),
        in_specs=[SMEM, SMEM],
        out_specs=(SMEM, SMEM),
        scratch_shapes=[pltpu.SMEM((groups,), jnp.int32)],
        name="route",
    )(listed.reshape(pairs), page_slot)
    arrived = lax.all_to_all(table.reshape(groups, capacity), "index", split_axis=0, concat_axis=0, tiled=True)

    pieces = gather_queries(queries, index % 2)

    order, slot_pad, slot_at, block_page, block_at, block_count = pl.pallas_call(
        functools.partial(sort_kernel, capacity, pages, half, blocks),
        out_shape=(ints(blocks * BLOCK + slots), ints(blocks * BLOCK + slots), ints(slots), ints(blocks), ints(blocks), ints(1)),
        in_specs=[SMEM, SMEM],
        out_specs=(SMEM,) * 6,
        scratch_shapes=[pltpu.SMEM((pages + 1,), jnp.int32)] * 3,
        name="sort_pairs",
    )(arrived.reshape(slots), me)

    limits = counts - rep * part
    flat = [x.reshape((-1,) + x.shape[-2:]) for x, _ in pieces]
    places = [at * half for _, at in pieces]
    scale = 1.0 / (math.sqrt(feature) * TAU)
    vectors, peaks, totals = pl.pallas_call(
        functools.partial(pair_kernel, places, scale),
        out_shape=(
            jax.ShapeDtypeStruct((slots + 2 * BLOCK, query_len, feature), BF16),
            jax.ShapeDtypeStruct((blocks, rows), F32),
            jax.ShapeDtypeStruct((blocks, rows), F32),
        ),
        in_specs=[SMEM] * 5 + [ANY] * (1 + len(flat)),
        out_specs=(VMEM, VMEM, VMEM),
        scratch_shapes=[
            pltpu.VMEM((groups * query_count, query_len, feature), BF16),
            pltpu.VMEM((pages, part, feature), BF16),
            pltpu.SemaphoreType.DMA((len(flat) + 1,)),
        ],
        compiler_params=params(48),
        name="pairs",
    )(order, block_page, block_at, block_count, limits, page_store, *flat)

    def rep_pairs(step):
        return [(i, (i + step) % reps) for i in range(reps)]

    stats = jnp.stack([peaks, totals])
    everyone = [stats] + [lax.ppermute(stats, "rep", rep_pairs(s)) for s in (1, -1, 2)]
    length = slots // 2 * share
    results = pl.pallas_call(
        functools.partial(scale_kernel, math.sqrt(feature)),
        out_shape=(jax.ShapeDtypeStruct((length, feature), BF16),) * 8 + (jax.ShapeDtypeStruct((slots // 128, 128), F32),),
        in_specs=[SMEM] * 3 + [VMEM] * 10,
        out_specs=(VMEM,) * 9,
        scratch_shapes=[
            pltpu.VMEM((blocks, rows), F32),
            pltpu.VMEM((blocks, rows), F32),
            pltpu.VMEM((4, (slots + 2 * BLOCK) * share, feature), F32),
        ],
        compiler_params=params(48),
        name="scale",
    )(
        block_at,
        block_count,
        me,
        slot_pad[: blocks * BLOCK].reshape(blocks, BLOCK),
        *[s[0] for s in everyone],
        *[s[1] for s in everyone],
        vectors,
    )
    scores = results[8]
    back = lax.all_to_all(scores.reshape(groups, capacity), "index", split_axis=0, concat_axis=0, tiled=True)
    pair_scores = back.reshape(slots)[place].reshape(query_count, list_len)
    highest = jnp.max(pair_scores, axis=1, keepdims=True)
    log_total = highest[:, 0] + jnp.log(jnp.sum(jnp.exp(pair_scores - highest), axis=1))
    losses = log_total - pair_scores[:, 0]
    probability = jnp.exp(pair_scores - log_total[:, None])
    target = (jnp.arange(list_len) == 0).astype(F32)
    coefficient = LOSS_SCALE * (probability - target[None, :])

    def travel(h, step, turn):
        held = results[turn[0] * 2 + h]
        for p in turn[1:3]:
            held = lax.ppermute(held, "rep", rep_pairs(step))
            held = (held.astype(F32) + results[p * 2 + h].astype(F32)).astype(BF16)
        return lax.ppermute(held, "rep", rep_pairs(step))

    in_a = travel(0, 1, (3, 2, 1))
    in_b = travel(1, -1, (1, 2, 3))
    outgoing = pl.pallas_call(
        functools.partial(slot_kernel, share),
        out_shape=jax.ShapeDtypeStruct((slots * share, feature), BF16),
        in_specs=[SMEM] + [VMEM] * 4,
        out_specs=VMEM,
        scratch_shapes=[pltpu.VMEM((slots * share, feature), F32)],
        compiler_params=params(32),
        name="slots",
    )(slot_at, in_a, results[0], in_b, results[1])
    returned = lax.all_to_all(
        outgoing.reshape(groups, capacity * share, feature), "index", split_axis=0, concat_axis=0, tiled=True
    )
    quarter = pl.pallas_call(
        functools.partial(gradient_kernel, share, list_len),
        out_shape=jax.ShapeDtypeStruct((query_count * share, feature), BF16),
        in_specs=[SMEM, SMEM, VMEM],
        out_specs=VMEM,
        scratch_shapes=[pltpu.VMEM((slots * share, feature), F32)],
        compiler_params=params(32),
        name="gradients",
    )(place, coefficient.reshape(pairs), returned.reshape(slots * share, feature))
    gathered = lax.all_gather(quarter.reshape(query_count, share, feature), "rep")
    gradients = jnp.transpose(gathered, (1, 0, 2, 3)).reshape(query_count, query_len, feature)
    return (losses, gradients)


def solution(mesh):
    return jax.shard_map(
        per_device,
        mesh=mesh,
        in_specs=(
            P("index", None, None),
            P("index", None),
            P(),
            P("index"),
            P("index", "rep", None),
        ),
        out_specs=(P("index"), P("index", None, None)),
        check_vma=False,
    )
```

```python
import functools
import math

import jax
import jax.numpy as jnp
from jax import lax
from jax.experimental import pallas as pl
from jax.experimental.pallas import tpu as pltpu
from jax.sharding import PartitionSpec as P

TAU = 0.1
LOSS_SCALE = 32.0
NEG = -1e30
BLOCK = 4
UNROLL = 16
CHUNKS = 2
LANES = 128
STRIDE = 256
PIECES = 3
RING = 4
F32 = jnp.float32
BF16 = jnp.bfloat16

SMEM = pl.BlockSpec(memory_space=pltpu.SMEM)
VMEM = pl.BlockSpec(memory_space=pltpu.VMEM)
ANY = pl.BlockSpec(memory_space=pl.ANY)


def params(mib):
    return pltpu.CompilerParams(vmem_limit_bytes=mib * 1024 * 1024)


def place_of(z, y, core):
    return ((z % RING) * RING + (y % RING)) * 2 + core


def ring_pairs(second, step):
    pairs = []
    for z in range(RING):
        for y in range(RING):
            for core in range(2):
                if (core == 0) != second:
                    there = place_of(z, y + step, core)
                else:
                    there = place_of(z + step, y, core)
                pairs.append((place_of(z, y, core), there))
    return pairs


CORE_PAIRS = [(i, i ^ 1) for i in range(2 * RING * RING)]


def across(x):
    return lax.ppermute(x, "index", CORE_PAIRS)


def gather_queries(queries, core):
    half = queries.shape[0] // 2
    keep = lax.dynamic_slice_in_dim(queries, core * half, half, 0)
    give = lax.dynamic_slice_in_dim(queries, (1 - core) * half, half, 0)
    got = across(give)
    own = jnp.where(core == 0, jnp.stack([keep, got]), jnp.stack([got, keep]))

    def spread(x, second):
        n = x.shape[0] // 2
        right = lax.ppermute(x, "index", ring_pairs(second, 1))
        left = lax.ppermute(x, "index", ring_pairs(second, -1))
        far_a = lax.ppermute(right[:n], "index", ring_pairs(second, 1))
        far_b = lax.ppermute(left[n:], "index", ring_pairs(second, -1))
        return right, left, far_a, far_b

    right, left, far_a, far_b = spread(own, False)
    own_spread = spread(own, True)
    rest = jnp.concatenate([right, left, far_a, far_b], axis=0)
    rest_spread = spread(rest, True)
    pieces = []
    for p, x in enumerate((own, own_spread[0], own_spread[1])):
        pieces.append((x, 8 * p))
    pieces.append((own_spread[2], 24))
    pieces.append((own_spread[3], 25))
    for p, x in enumerate((rest, rest_spread[0], rest_spread[1])):
        pieces.append((x, 8 * p + 2))
    pieces.append((rest_spread[2], 26))
    pieces.append((rest_spread[3], 29))
    swapped = [(across(x), 32 + at) for x, at in pieces]
    return pieces + swapped


def route_kernel(capacity, page_bits, list_len, listed, page_slot, table, place, used):
    slots = table.shape[0]
    pairs = listed.shape[0]
    groups = used.shape[0]
    sub = capacity // CHUNKS

    def clear(i, _):
        for k in range(16):
            table[i * 16 + k] = -1
        return 0

    lax.fori_loop(0, slots // 16, clear, 0)
    for i in range(groups):
        used[i] = 0

    def step(q, _):
        for k in range(list_len):
            i = q * list_len + k
            row = page_slot[listed[i]]
            owner = lax.shift_right_logical(row, page_bits)
            n = jnp.minimum(used[owner], capacity - 1)
            used[owner] = n + 1
            chunk = n & 1
            j = lax.shift_right_logical(n, 1)
            table[owner * capacity + chunk * sub + j] = lax.shift_left(q, page_bits) + (row & ((1 << page_bits) - 1))
            place[i] = chunk * (groups * sub) + owner * sub + j
        return 0

    lax.fori_loop(0, pairs // list_len, step, 0)


def sort_kernel(capacity, page_bits, half, blocks, arrived, me, order, block_page, block_count, count, first):
    slots = arrived.shape[0]
    groups = slots // capacity
    sub = capacity // CHUNKS
    pages = 1 << page_bits
    z = lax.shift_right_logical(me[0], 3)
    y = lax.shift_right_logical(me[0], 1) & (RING - 1)
    core = me[0] & 1
    nothing = (groups // 2) * sub * 2048

    def clear(i, _):
        for k in range(16):
            order[i * 16 + k] = nothing
        return 0

    lax.fori_loop(0, CHUNKS * blocks * BLOCK // 16, clear, 0)

    def clear_blocks(i, _):
        for k in range(16):
            block_page[i * 16 + k] = 0
        return 0

    lax.fori_loop(0, CHUNKS * blocks // 16, clear_blocks, 0)
    for i in range(CHUNKS * pages + 1):
        count[i] = 0

    def tally(s, _):
        for chunk in range(CHUNKS):
            for j in range(sub):
                code = arrived[s * capacity + chunk * sub + j]
                p = jnp.where(code < 0, CHUNKS * pages, (code & (pages - 1)) + chunk * pages)
                count[p] = count[p] + 1
        return 0

    lax.fori_loop(0, groups, tally, 0)

    for chunk in range(CHUNKS):

        def lay(p, b):
            n = count[chunk * pages + p]
            first[chunk * pages + p] = b * BLOCK
            count[chunk * pages + p] = 0
            steps = lax.shift_right_logical(n + BLOCK - 1, 2)

            def one(k, _):
                block_page[b + k] = p
                return 0

            lax.fori_loop(0, steps, one, 0)
            return b + steps

        total = lax.fori_loop(0, pages, lay, jnp.int32(chunk * blocks))
        block_count[chunk] = total - chunk * blocks
    first[CHUNKS * pages] = CHUNKS * blocks * BLOCK
    count[CHUNKS * pages] = 0

    def rank(there, mine):
        apart = (there - mine) & (RING - 1)
        return jnp.where(apart == 0, 0, jnp.where(apart == RING - 1, 1, jnp.where(apart == 1, 2, 3)))

    def source(s, _):
        dz = rank(lax.shift_right_logical(s, 3), z)
        dy = rank(lax.shift_right_logical(s, 1) & (RING - 1), y)
        sc = s & 1
        low = ((jnp.where(core == 0, 0, RING) + dz) * RING + dy) * 2 + sc
        high = ((jnp.where(core == 1, 0, RING) + dy) * RING + dz) * 2 + sc
        side = lax.shift_right_logical(s, 4)
        slot = side * STRIDE + (s & 15) * sub
        low_base = low * half + slot * 2048
        high_base = high * half - half + slot * 2048
        for chunk in range(CHUNKS):
            for j in range(sub):
                code = arrived[s * capacity + chunk * sub + j]
                p = jnp.where(code < 0, CHUNKS * pages, (code & (pages - 1)) + chunk * pages)
                q = lax.shift_right_logical(jnp.maximum(code, 0), page_bits)
                r = count[p]
                count[p] = r + 1
                order[first[p] + r] = q + jnp.where(q < half, low_base, high_base) + j * 2048
        return 0

    lax.fori_loop(0, groups, source, 0)


def split(x):
    parts = []
    for _ in range(PIECES):
        part = x.astype(BF16)
        parts.append(part)
        x = x - part.astype(F32)
    return parts


def pair_kernel(chunk, blocks, places, scale, order, block_page, block_count, limits, me, *refs):
    n_pieces = len(places)
    store = refs[0]
    pieces = refs[1 : 1 + n_pieces]
    outs = refs[1 + n_pieces : 9 + n_pieces]
    held, pages, wide, stats, sems = refs[9 + n_pieces :]
    copies = [pltpu.make_async_copy(store, pages, sems.at[n_pieces])]
    for k, (ref, at) in enumerate(zip(pieces, places, strict=True)):
        copies.append(pltpu.make_async_copy(ref, held.at[pl.ds(at, ref.shape[0])], sems.at[k]))
    for c in copies:
        c.start()
    for c in copies:
        c.wait()
    part = pages.shape[1]
    tokens = held.shape[1]
    share = tokens // 4
    power = scale * math.log2(math.e)
    lane = lax.broadcasted_iota(jnp.int32, (1, part), 1)
    lanes = lax.broadcasted_iota(jnp.int32, (tokens, LANES), 1)

    def step(it, _):
        for u in range(UNROLL):
            b = chunk * blocks + it * UNROLL + u
            p = block_page[b]
            codes = [order[b * BLOCK + i] for i in range(BLOCK)]
            block = jnp.concatenate([held[c & 2047] for c in codes], axis=0)
            page = pages[p]
            raw = lax.dot_general(block, page, (((1,), (1,)), ((), ())), preferred_element_type=F32)
            raw = jnp.where(lane < limits[p], raw, NEG)
            top = jnp.max(raw, axis=1, keepdims=True)
            weights = jnp.exp2((raw - top) * power)
            total = jnp.sum(weights, axis=1, keepdims=True)
            out = jnp.dot(weights.astype(BF16), page, preferred_element_type=F32)
            peak = jnp.maximum(top * scale, NEG)
            for i in range(BLOCK):
                slot = lax.shift_right_logical(codes[i], 11)
                for t in range(4):
                    first = i * tokens + t * share
                    wide[t, pl.ds(pl.multiple_of(slot * share, share), share), :] = out[first : first + share]
                here = lanes == (slot & (LANES - 1))
                at = lax.shift_right_logical(slot, 7)
                rows = slice(i * tokens, (i + 1) * tokens)
                stats[0, at] = jnp.where(here, peak[rows], stats[0, at])
                stats[1, at] = jnp.where(here, total[rows], stats[1, at])
        return 0

    lax.fori_loop(0, (block_count[chunk] + UNROLL - 1) // UNROLL, step, 0)

    rep = me[1]
    length = outs[0].shape[0] - 2 * PIECES * 2 * share
    piece = 128
    for p in range(4):
        t = (rep + p) & 3
        for h in range(2):
            out = outs[p * 2 + h]

            def narrow(i, _):
                at = pl.multiple_of(i * piece, piece)
                out[pl.ds(at, piece), :] = wide[t, pl.ds(at + h * STRIDE * share, piece), :].astype(BF16)
                return 0

            lax.fori_loop(0, length // piece, narrow, 0)
            for s in range(2):
                rows = pl.ds(pl.multiple_of(t * share, share), share)
                both = jnp.concatenate([stats[s, h * 2, rows, :], stats[s, h * 2 + 1, rows, :]], axis=0)
                for k, x in enumerate(split(both)):
                    at = length + (s * PIECES + k) * 2 * share
                    out[at : at + 2 * share, :] = x


def merge_kernel(last, root, share, *refs):
    ins = refs[:4]
    outs = refs[4:]
    length = ins[0].shape[0] - 2 * PIECES * 2 * share
    for h in range(2):
        came, own = ins[2 * h], ins[2 * h + 1]

        def joined(ref, s):
            at = length + s * PIECES * 2 * share
            tiles = [ref[at + k * 2 * share : at + (k + 1) * 2 * share, :].astype(F32) for k in range(PIECES)]
            return tiles[0] + (tiles[1] + tiles[2])

        peak_a, total_a, peak_b, total_b = joined(came, 0), joined(came, 1), joined(own, 0), joined(own, 1)
        peak = jnp.maximum(peak_a, peak_b)
        part_a, part_b = jnp.exp(peak_a - peak), jnp.exp(peak_b - peak)
        total = total_a * part_a + total_b * part_b
        if last:
            part_a, part_b = part_a / (total * root), part_b / (total * root)
            logs = TAU * (peak + jnp.log(total))
            for k in range(2):
                row = jnp.sum(logs[k * share : (k + 1) * share], axis=0, keepdims=True)
                outs[1][2 * h + k : 2 * h + k + 1, :] = row
            out, base = outs[0], h * length
        else:
            out, base = outs[h], 0
            for s, x in enumerate((peak, total)):
                for k, tile in enumerate(split(x)):
                    at = length + (s * PIECES + k) * 2 * share
                    out[at : at + 2 * share, :] = tile
        for pair in range(length // (2 * share)):
            at = pair * 2 * share

            def factor(x):
                columns = []
                for slot in (2 * pair, 2 * pair + 1):
                    k, n = slot // LANES, slot % LANES
                    columns.append(jnp.broadcast_to(x[k * share : (k + 1) * share, n : n + 1], (share, LANES)))
                return jnp.concatenate(columns, axis=0)

            rows = slice(at, at + 2 * share)
            value = came[rows, :].astype(F32) * factor(part_a) + own[rows, :].astype(F32) * factor(part_b)
            out[base + at : base + at + 2 * share, :] = value.astype(BF16)


def gradient_kernel(share, list_len, place, weight, first, second, out, wide):
    length = first.shape[0]
    for h, x in enumerate((first, second)):

        def widen(i, _):
            at = pl.multiple_of(i * 128, 128)
            wide[pl.ds(h * length + at, 128), :] = x[pl.ds(at, 128), :].astype(F32)
            return 0

        lax.fori_loop(0, length // 128, widen, 0)

    def step(i, _):
        parts = []
        for s in range(2):
            total = jnp.zeros((share, out.shape[1]), F32)
            for k in range(list_len):
                e = (i * 2 + s) * list_len + k
                at = pl.multiple_of(place[e] * share, share)
                total = total + weight[e] * wide[pl.ds(at, share), :]
            parts.append(total)
        out[pl.ds(pl.multiple_of(i * 2 * share, 2 * share), 2 * share), :] = jnp.concatenate(parts, axis=0).astype(BF16)
        return 0

    lax.fori_loop(0, out.shape[0] // share // 2, step, 0)


def ints(*shape):
    return jax.ShapeDtypeStruct(shape, jnp.int32)


def per_device(queries, listed, page_slot, counts, page_store):
    groups = lax.axis_size("index")
    index = lax.axis_index("index").astype(jnp.int32)
    rep = lax.axis_index("rep").astype(jnp.int32)
    reps = lax.axis_size("rep")
    query_count, query_len, feature = queries.shape
    list_len = listed.shape[1]
    pages, part, _ = page_store.shape
    page_bits = pages.bit_length() - 1
    pairs = query_count * list_len
    capacity = 2 * pairs // groups
    sub = capacity // CHUNKS
    slots = groups * capacity
    half = query_count // 2
    share = query_len // reps
    blocks = (groups * sub + (BLOCK - 1) * pages) // BLOCK
    blocks = (blocks + UNROLL - 1) // UNROLL * UNROLL
    me = jnp.stack([index, rep])
    root = math.sqrt(feature)
    scale = 1.0 / (root * TAU)

    table, place = pl.pallas_call(
        functools.partial(route_kernel, capacity, page_bits, list_len),
        out_shape=(ints(slots), ints(pairs)),
        in_specs=[SMEM, SMEM],
        out_specs=(SMEM, SMEM),
        scratch_shapes=[pltpu.SMEM((groups,), jnp.int32)],
        name="route",
    )(listed.reshape(pairs), page_slot)
    arrived = lax.all_to_all(table.reshape(groups, capacity), "index", split_axis=0, concat_axis=0, tiled=True)

    pieces = gather_queries(queries, index % 2)

    order, block_page, block_count = pl.pallas_call(
        functools.partial(sort_kernel, capacity, page_bits, half, blocks),
        out_shape=(ints(CHUNKS * blocks * BLOCK + slots), ints(CHUNKS * blocks), ints(CHUNKS)),
        in_specs=[SMEM, SMEM],
        out_specs=(SMEM,) * 3,
        scratch_shapes=[pltpu.SMEM((CHUNKS * pages + 1,), jnp.int32)] * 2,
        cost_estimate=pl.CostEstimate(flops=0, bytes_accessed=40_000_000, transcendentals=0),
        name="sort_pairs",
    )(arrived.reshape(slots), me)

    limits = counts - rep * part
    flat = [x.reshape((-1,) + x.shape[-2:]) for x, _ in pieces]
    places = [at * half for _, at in pieces]

    length = groups // 2 * sub * share
    packed = length + 2 * PIECES * 2 * share

    def rep_pairs(step):
        return [(i, (i + step) % reps) for i in range(reps)]

    def travel(x, step):
        return lax.ppermute(x, "rep", rep_pairs(step))

    returned, scores = [], []
    for chunk in range(CHUNKS):
        parts = pl.pallas_call(
            functools.partial(pair_kernel, chunk, blocks, places, scale),
            out_shape=(jax.ShapeDtypeStruct((packed, feature), BF16),) * 8,
            in_specs=[SMEM] * 5 + [ANY] * (1 + len(flat)),
            out_specs=(VMEM,) * 8,
            scratch_shapes=[
                pltpu.VMEM((groups * query_count, query_len, feature), BF16),
                pltpu.VMEM((pages, part, feature), BF16),
                pltpu.VMEM((4, 2 * STRIDE * share, feature), F32),
                pltpu.VMEM((2, 2 * STRIDE // LANES, query_len, LANES), F32),
                pltpu.SemaphoreType.DMA((len(flat) + 1,)),
            ],
            compiler_params=params(48),
            cost_estimate=pl.CostEstimate(flops=0, bytes_accessed=60_000_000, transcendentals=0),
            name="pairs",
        )(order, block_page, block_count, limits, me, page_store, *flat)

        held = [parts[3 * 2], parts[1 * 2 + 1]]
        for hop in range(3):
            came = [travel(held[0], 1), travel(held[1], -1)]
            own = [parts[(2, 1, 0)[hop] * 2], parts[(2, 3, 0)[hop] * 2 + 1]]
            last = hop == 2
            if last:
                out_shape = (jax.ShapeDtypeStruct((2 * length, feature), BF16), jax.ShapeDtypeStruct((4, LANES), F32))
            else:
                out_shape = (jax.ShapeDtypeStruct((packed, feature), BF16),) * 2
            held = pl.pallas_call(
                functools.partial(merge_kernel, last, root, share),
                out_shape=out_shape,
                in_specs=[VMEM] * 4,
                out_specs=(VMEM,) * 2,
                compiler_params=params(24),
                cost_estimate=pl.CostEstimate(flops=0, bytes_accessed=8_000_000, transcendentals=0),
                name="merge",
            )(came[0], own[0], came[1], own[1])
        directions, logs = held
        returned.append(
            lax.all_to_all(directions.reshape(groups, sub * share, feature), "index", split_axis=0, concat_axis=0, tiled=True)
        )
        logs = logs + travel(logs, 1) + travel(logs, -1) + travel(logs, 2)
        logs = logs.reshape(2, STRIDE)[:, : groups // 2 * sub].reshape(groups, sub)
        scores.append(lax.all_to_all(logs, "index", split_axis=0, concat_axis=0, tiled=True))

    pair_scores = jnp.stack(scores).reshape(slots)[place].reshape(query_count, list_len)
    highest = jnp.max(pair_scores, axis=1, keepdims=True)
    log_total = highest[:, 0] + jnp.log(jnp.sum(jnp.exp(pair_scores - highest), axis=1))
    losses = log_total - pair_scores[:, 0]
    probability = jnp.exp(pair_scores - log_total[:, None])
    target = (jnp.arange(list_len) == 0).astype(F32)
    coefficient = LOSS_SCALE * (probability - target[None, :])

    quarter = pl.pallas_call(
        functools.partial(gradient_kernel, share, list_len),
        out_shape=jax.ShapeDtypeStruct((query_count * share, feature), BF16),
        in_specs=[SMEM, SMEM, VMEM, VMEM],
        out_specs=VMEM,
        scratch_shapes=[pltpu.VMEM((slots * share, feature), F32)],
        compiler_params=params(32),
        name="gradients",
    )(place, coefficient.reshape(pairs), *[x.reshape(-1, feature) for x in returned])
    gathered = lax.all_gather(quarter.reshape(query_count, share, feature), "rep")
    gradients = jnp.transpose(gathered, (1, 0, 2, 3)).reshape(query_count, query_len, feature)
    return (losses, gradients)


def solution(mesh):
    return jax.shard_map(
        per_device,
        mesh=mesh,
        in_specs=(
            P("index", None, None),
            P("index", None),
            P(),
            P("index"),
            P("index", "rep", None),
        ),
        out_specs=(P("index"), P("index", None, None)),
        check_vma=False,
    )
```

```python
import functools
import math

import jax
import jax.numpy as jnp
from jax import lax
from jax.experimental import pallas as pl
from jax.experimental.pallas import tpu as pltpu
from jax.sharding import PartitionSpec as P

TAU = 0.1
LOSS_SCALE = 32.0
NEG = -1e30
BLOCK = 4
UNROLL = 16
CHUNKS = 2
LANES = 128
STRIDE = 256
PIECES = 3
F32 = jnp.float32
BF16 = jnp.bfloat16

SMEM = pl.BlockSpec(memory_space=pltpu.SMEM)
VMEM = pl.BlockSpec(memory_space=pltpu.VMEM)
ANY = pl.BlockSpec(memory_space=pl.ANY)


def params(mib):
    return pltpu.CompilerParams(vmem_limit_bytes=mib * 1024 * 1024)


def route_kernel(capacity, page_bits, list_len, listed, page_slot, table, place, tile, used):
    slots = table.shape[0]
    pairs = listed.shape[0]
    groups = used.shape[0]
    sub = capacity // CHUNKS

    def clear(i, _):
        for k in range(16):
            table[i * 16 + k] = -1
        return 0

    lax.fori_loop(0, slots // 16, clear, 0)
    for i in range(groups):
        used[i] = 0

    def step(q, _):
        for k in range(list_len):
            i = q * list_len + k
            row = page_slot[listed[i]]
            owner = lax.shift_right_logical(row, page_bits)
            n = jnp.minimum(used[owner], capacity - 1)
            used[owner] = n + 1
            chunk = n & 1
            j = lax.shift_right_logical(n, 1)
            table[owner * capacity + chunk * sub + j] = lax.shift_left(q, page_bits) + (row & ((1 << page_bits) - 1))
            place[i] = owner * capacity + chunk * sub + j
            tile[i] = owner * (capacity + 2) + chunk * sub + j
        return 0

    lax.fori_loop(0, pairs // list_len, step, 0)


def sort_kernel(capacity, page_bits, query_count, blocks, arrived, order, block_page, block_count, count, first):
    slots = arrived.shape[0]
    groups = slots // capacity
    sub = capacity // CHUNKS
    pages = 1 << page_bits
    nothing = (groups // 2) * sub * 2048

    def clear(i, _):
        for k in range(16):
            order[i * 16 + k] = nothing
        return 0

    lax.fori_loop(0, CHUNKS * blocks * BLOCK // 16, clear, 0)

    def clear_blocks(i, _):
        for k in range(16):
            block_page[i * 16 + k] = 0
        return 0

    lax.fori_loop(0, CHUNKS * blocks // 16, clear_blocks, 0)
    for i in range(CHUNKS * pages + 1):
        count[i] = 0

    def tally(s, _):
        for chunk in range(CHUNKS):
            for j in range(sub):
                code = arrived[s * capacity + chunk * sub + j]
                p = jnp.where(code < 0, CHUNKS * pages, (code & (pages - 1)) + chunk * pages)
                count[p] = count[p] + 1
        return 0

    lax.fori_loop(0, groups, tally, 0)

    for chunk in range(CHUNKS):

        def lay(p, b):
            n = count[chunk * pages + p]
            first[chunk * pages + p] = b * BLOCK
            count[chunk * pages + p] = 0
            steps = lax.shift_right_logical(n + BLOCK - 1, 2)

            def one(k, _):
                block_page[b + k] = p
                return 0

            lax.fori_loop(0, steps, one, 0)
            return b + steps

        total = lax.fori_loop(0, pages, lay, jnp.int32(chunk * blocks))
        block_count[chunk] = total - chunk * blocks
    first[CHUNKS * pages] = CHUNKS * blocks * BLOCK
    count[CHUNKS * pages] = 0

    def source(s, _):
        side = lax.shift_right_logical(s, 4)
        slot = side * STRIDE + (s & 15) * sub
        base = s * query_count + slot * 2048
        for chunk in range(CHUNKS):
            for j in range(sub):
                code = arrived[s * capacity + chunk * sub + j]
                p = jnp.where(code < 0, CHUNKS * pages, (code & (pages - 1)) + chunk * pages)
                q = lax.shift_right_logical(jnp.maximum(code, 0), page_bits)
                r = count[p]
                count[p] = r + 1
                order[first[p] + r] = q + base + j * 2048
        return 0

    lax.fori_loop(0, groups, source, 0)


def split(x):
    parts = []
    for _ in range(PIECES):
        part = x.astype(BF16)
        parts.append(part)
        x = x - part.astype(F32)
    return parts


def pair_kernel(chunk, blocks, scale, order, block_page, block_count, limits, me, *refs):
    store, queries = refs[:2]
    outs = refs[2:10]
    held, pages, wide, stats, sems = refs[10:]
    copies = [pltpu.make_async_copy(queries, held, sems.at[0]), pltpu.make_async_copy(store, pages, sems.at[1])]
    for c in copies:
        c.start()
    for c in copies:
        c.wait()
    part = pages.shape[1]
    tokens = held.shape[1]
    share = tokens // 4
    power = scale * math.log2(math.e)
    lane = lax.broadcasted_iota(jnp.int32, (1, part), 1)
    lanes = lax.broadcasted_iota(jnp.int32, (tokens, LANES), 1)

    def step(it, _):
        for u in range(UNROLL):
            b = chunk * blocks + it * UNROLL + u
            p = block_page[b]
            codes = [order[b * BLOCK + i] for i in range(BLOCK)]
            block = jnp.concatenate([held[c & 2047] for c in codes], axis=0)
            page = pages[p]
            raw = lax.dot_general(block, page, (((1,), (1,)), ((), ())), preferred_element_type=F32)
            raw = jnp.where(lane < limits[p], raw, NEG)
            top = jnp.max(raw, axis=1, keepdims=True)
            weights = jnp.exp2((raw - top) * power)
            total = jnp.sum(weights, axis=1, keepdims=True)
            out = jnp.dot(weights.astype(BF16), page, preferred_element_type=F32)
            peak = jnp.maximum(top * scale, NEG)
            for i in range(BLOCK):
                slot = lax.shift_right_logical(codes[i], 11)
                for t in range(4):
                    first = i * tokens + t * share
                    wide[t, pl.ds(pl.multiple_of(slot * share, share), share), :] = out[first : first + share]
                here = lanes == (slot & (LANES - 1))
                at = lax.shift_right_logical(slot, 7)
                rows = slice(i * tokens, (i + 1) * tokens)
                stats[0, at] = jnp.where(here, peak[rows], stats[0, at])
                stats[1, at] = jnp.where(here, total[rows], stats[1, at])
        return 0

    lax.fori_loop(0, (block_count[chunk] + UNROLL - 1) // UNROLL, step, 0)

    rep = me[0]
    length = outs[0].shape[0] - 2 * PIECES * 2 * share
    piece = 128
    for p in range(4):
        t = (rep + p) & 3
        for h in range(2):
            out = outs[p * 2 + h]

            def narrow(i, _):
                at = pl.multiple_of(i * piece, piece)
                out[pl.ds(at, piece), :] = wide[t, pl.ds(at + h * STRIDE * share, piece), :].astype(BF16)
                return 0

            lax.fori_loop(0, length // piece, narrow, 0)
            for s in range(2):
                rows = pl.ds(pl.multiple_of(t * share, share), share)
                both = jnp.concatenate([stats[s, h * 2, rows, :], stats[s, h * 2 + 1, rows, :]], axis=0)
                for k, x in enumerate(split(both)):
                    at = length + (s * PIECES + k) * 2 * share
                    out[at : at + 2 * share, :] = x


def merge_kernel(last, root, share, sub, *refs):
    n_in = 4 * CHUNKS if last else 4
    ins = refs[:n_in]
    outs = refs[n_in:]
    length = ins[0].shape[0] - 2 * PIECES * 2 * share
    span = 2 * sub * share + 2 * share
    for n in range(n_in // 2):
        chunk, h = n // 2, n % 2
        came, own = ins[2 * n], ins[2 * n + 1]

        def joined(ref, s):
            at = length + s * PIECES * 2 * share
            tiles = [ref[at + k * 2 * share : at + (k + 1) * 2 * share, :].astype(F32) for k in range(PIECES)]
            return tiles[0] + (tiles[1] + tiles[2])

        peak_a, total_a, peak_b, total_b = joined(came, 0), joined(came, 1), joined(own, 0), joined(own, 1)
        peak = jnp.maximum(peak_a, peak_b)
        part_a, part_b = jnp.exp(peak_a - peak), jnp.exp(peak_b - peak)
        total = total_a * part_a + total_b * part_b
        if last:
            part_a, part_b = part_a / (total * root), part_b / (total * root)
            logs = TAU * (peak + jnp.log(total))
            rows = [jnp.sum(logs[k * share : (k + 1) * share], axis=0, keepdims=True) for k in range(2)]
            if chunk == 0:
                kept = {**(kept if h else {}), h: rows}
            else:
                both = jnp.concatenate(kept[h] + rows, axis=0)
                tile = jnp.concatenate([x.astype(F32) for x in split(both)] + [both * 0.0], axis=0).astype(BF16)
                sources = length // (sub * share)
                for source in range(sources):
                    at = (h * sources + source) * span + 2 * sub * share
                    outs[0][at : at + 2 * share, :] = tile
        else:
            for s, x in enumerate((peak, total)):
                for k, tile in enumerate(split(x)):
                    at = length + (s * PIECES + k) * 2 * share
                    outs[h][at : at + 2 * share, :] = tile
        for pair in range(length // (2 * share)):
            at = pair * 2 * share

            def factor(x):
                columns = []
                for slot in (2 * pair, 2 * pair + 1):
                    k, lane = slot // LANES, slot % LANES
                    columns.append(jnp.broadcast_to(x[k * share : (k + 1) * share, lane : lane + 1], (share, LANES)))
                return jnp.concatenate(columns, axis=0)

            rows = slice(at, at + 2 * share)
            value = came[rows, :].astype(F32) * factor(part_a) + own[rows, :].astype(F32) * factor(part_b)
            if last:
                source, j = 2 * pair // sub, 2 * pair % sub
                to = (h * (length // (sub * share)) + source) * span + (chunk * sub + j) * share
                outs[0][to : to + 2 * share, :] = value.astype(BF16)
            else:
                outs[h][rows, :] = value.astype(BF16)


def gradient_kernel(share, list_len, place, weight, directions, out, wide):
    def widen(i, _):
        at = pl.multiple_of(i * 128, 128)
        wide[pl.ds(at, 128), :] = directions[pl.ds(at, 128), :].astype(F32)
        return 0

    lax.fori_loop(0, directions.shape[0] // 128, widen, 0)

    def step(i, _):
        parts = []
        for s in range(2):
            total = jnp.zeros((share, out.shape[1]), F32)
            for k in range(list_len):
                e = (i * 2 + s) * list_len + k
                at = pl.multiple_of(place[e] * share, share)
                total = total + weight[e] * wide[pl.ds(at, share), :]
            parts.append(total)
        out[pl.ds(pl.multiple_of(i * 2 * share, 2 * share), 2 * share), :] = jnp.concatenate(parts, axis=0).astype(BF16)
        return 0

    lax.fori_loop(0, out.shape[0] // share // 2, step, 0)


def ints(*shape):
    return jax.ShapeDtypeStruct(shape, jnp.int32)


def per_device(queries, listed, page_slot, counts, page_store):
    groups = lax.axis_size("index")
    index = lax.axis_index("index").astype(jnp.int32)
    rep = lax.axis_index("rep").astype(jnp.int32)
    reps = lax.axis_size("rep")
    query_count, query_len, feature = queries.shape
    list_len = listed.shape[1]
    pages, part, _ = page_store.shape
    page_bits = pages.bit_length() - 1
    pairs = query_count * list_len
    capacity = 2 * pairs // groups
    sub = capacity // CHUNKS
    slots = groups * capacity
    share = query_len // reps
    blocks = (groups * sub + (BLOCK - 1) * pages) // BLOCK
    blocks = (blocks + UNROLL - 1) // UNROLL * UNROLL
    root = math.sqrt(feature)
    scale = 1.0 / (root * TAU)

    table, place, tile = pl.pallas_call(
        functools.partial(route_kernel, capacity, page_bits, list_len),
        out_shape=(ints(slots), ints(pairs), ints(pairs)),
        in_specs=[SMEM, SMEM],
        out_specs=(SMEM,) * 3,
        scratch_shapes=[pltpu.SMEM((groups,), jnp.int32)],
        name="route",
    )(listed.reshape(pairs), page_slot)
    arrived = lax.all_to_all(table.reshape(groups, capacity), "index", split_axis=0, concat_axis=0, tiled=True)

    everyone = lax.all_gather(queries, "index", tiled=True)

    order, block_page, block_count = pl.pallas_call(
        functools.partial(sort_kernel, capacity, page_bits, query_count, blocks),
        out_shape=(ints(CHUNKS * blocks * BLOCK + slots), ints(CHUNKS * blocks), ints(CHUNKS)),
        in_specs=[SMEM],
        out_specs=(SMEM,) * 3,
        scratch_shapes=[pltpu.SMEM((CHUNKS * pages + 1,), jnp.int32)] * 2,
        cost_estimate=pl.CostEstimate(flops=0, bytes_accessed=40_000_000, transcendentals=0),
        name="sort_pairs",
    )(arrived.reshape(slots))

    limits = counts - rep * part
    me = rep[None]

    length = groups // 2 * sub * share
    packed = length + 2 * PIECES * 2 * share

    def rep_pairs(step):
        return [(i, (i + step) % reps) for i in range(reps)]

    def travel(x, step):
        return lax.ppermute(x, "rep", rep_pairs(step))

    finals = []
    for chunk in range(CHUNKS):
        parts = pl.pallas_call(
            functools.partial(pair_kernel, chunk, blocks, scale),
            out_shape=(jax.ShapeDtypeStruct((packed, feature), BF16),) * 8,
            in_specs=[SMEM] * 5 + [ANY] * 2,
            out_specs=(VMEM,) * 8,
            scratch_shapes=[
                pltpu.VMEM((groups * query_count, query_len, feature), BF16),
                pltpu.VMEM((pages, part, feature), BF16),
                pltpu.VMEM((4, 2 * STRIDE * share, feature), F32),
                pltpu.VMEM((2, 2 * STRIDE // LANES, query_len, LANES), F32),
                pltpu.SemaphoreType.DMA((2,)),
            ],
            compiler_params=params(48),
            cost_estimate=pl.CostEstimate(flops=0, bytes_accessed=60_000_000, transcendentals=0),
            name="pairs",
        )(order, block_page, block_count, limits, me, page_store, everyone)

        held = [parts[3 * 2], parts[1 * 2 + 1]]
        for hop in range(3):
            came = [travel(held[0], 1), travel(held[1], -1)]
            own = [parts[(2, 1, 0)[hop] * 2], parts[(2, 3, 0)[hop] * 2 + 1]]
            if hop == 2:
                finals += [came[0], own[0], came[1], own[1]]
                break
            held = pl.pallas_call(
                functools.partial(merge_kernel, False, root, share, sub),
                out_shape=(jax.ShapeDtypeStruct((packed, feature), BF16),) * 2,
                in_specs=[VMEM] * 4,
                out_specs=(VMEM,) * 2,
                compiler_params=params(24),
                cost_estimate=pl.CostEstimate(flops=0, bytes_accessed=8_000_000, transcendentals=0),
                name="merge",
            )(came[0], own[0], came[1], own[1])
    span = 2 * sub * share + 2 * share
    outgoing = pl.pallas_call(
        functools.partial(merge_kernel, True, root, share, sub),
        out_shape=jax.ShapeDtypeStruct((groups * span, feature), BF16),
        in_specs=[VMEM] * (4 * CHUNKS),
        out_specs=VMEM,
        compiler_params=params(24),
        name="merge_last",
    )(*finals)
    returned = lax.all_to_all(outgoing.reshape(groups, span, feature), "index", split_axis=0, concat_axis=0, tiled=True)

    logs = returned[:, capacity * share : capacity * share + 4 * PIECES].astype(F32)
    logs = jnp.sum(logs.reshape(groups, PIECES, CHUNKS, STRIDE), axis=1)
    logs = lax.dynamic_slice_in_dim(logs, (index % (groups // 2)) * sub, sub, 2).reshape(slots)
    logs = logs + travel(logs, 1) + travel(logs, -1) + travel(logs, 2)
    pair_scores = logs[place].reshape(query_count, list_len)
    highest = jnp.max(pair_scores, axis=1, keepdims=True)
    log_total = highest[:, 0] + jnp.log(jnp.sum(jnp.exp(pair_scores - highest), axis=1))
    losses = log_total - pair_scores[:, 0]
    probability = jnp.exp(pair_scores - log_total[:, None])
    target = (jnp.arange(list_len) == 0).astype(F32)
    coefficient = LOSS_SCALE * (probability - target[None, :])

    quarter = pl.pallas_call(
        functools.partial(gradient_kernel, share, list_len),
        out_shape=jax.ShapeDtypeStruct((query_count * share, feature), BF16),
        in_specs=[SMEM, SMEM, VMEM],
        out_specs=VMEM,
        scratch_shapes=[pltpu.VMEM((groups * span, feature), F32)],
        compiler_params=params(32),
        name="gradients",
    )(tile, coefficient.reshape(pairs), returned.reshape(groups * span, feature))
    gathered = lax.all_gather(quarter.reshape(query_count, share, feature), "rep")
    gradients = jnp.transpose(gathered, (1, 0, 2, 3)).reshape(query_count, query_len, feature)
    return (losses, gradients)


def solution(mesh):
    return jax.shard_map(
        per_device,
        mesh=mesh,
        in_specs=(
            P("index", None, None),
            P("index", None),
            P(),
            P("index"),
            P("index", "rep", None),
        ),
        out_specs=(P("index"), P("index", None, None)),
        check_vma=False,
    )
```

```python
import functools
import math

import jax
import jax.numpy as jnp
from jax import lax
from jax.experimental import pallas as pl
from jax.experimental.pallas import tpu as pltpu
from jax.sharding import PartitionSpec as P

TAU = 0.1
LOSS_SCALE = 32.0
NEG = -1e30
BLOCK = 4
UNROLL = 16
CHUNKS = 2
LANES = 128
STRIDE = 256
PIECES = 3
F32 = jnp.float32
BF16 = jnp.bfloat16

SMEM = pl.BlockSpec(memory_space=pltpu.SMEM)
VMEM = pl.BlockSpec(memory_space=pltpu.VMEM)
ANY = pl.BlockSpec(memory_space=pl.ANY)


def params(mib):
    return pltpu.CompilerParams(vmem_limit_bytes=mib * 1024 * 1024)


def route_kernel(capacity, page_bits, list_len, listed, page_slot, table, place, tile, used):
    slots = table.shape[0]
    pairs = listed.shape[0]
    groups = used.shape[0]
    sub = capacity // CHUNKS

    def clear(i, _):
        for k in range(16):
            table[i * 16 + k] = -1
        return 0

    lax.fori_loop(0, slots // 16, clear, 0)
    for i in range(groups):
        used[i] = 0

    def step(q, _):
        for k in range(list_len):
            i = q * list_len + k
            row = page_slot[listed[i]]
            owner = lax.shift_right_logical(row, page_bits)
            n = jnp.minimum(used[owner], capacity - 1)
            used[owner] = n + 1
            chunk = n & 1
            j = lax.shift_right_logical(n, 1)
            table[owner * capacity + chunk * sub + j] = lax.shift_left(q, page_bits) + (row & ((1 << page_bits) - 1))
            place[i] = owner * capacity + chunk * sub + j
            tile[i] = owner * (capacity + 2) + chunk * sub + j
        return 0

    lax.fori_loop(0, pairs // list_len, step, 0)


def sort_kernel(capacity, page_bits, query_count, blocks, arrived, order, count, first):
    page_base = CHUNKS * blocks * BLOCK
    total_base = page_base + CHUNKS * blocks
    slots = arrived.shape[0]
    groups = slots // capacity
    sub = capacity // CHUNKS
    pages = 1 << page_bits
    nothing = (groups // 2) * sub * 2048

    def clear(i, _):
        for k in range(16):
            order[i * 16 + k] = nothing
        return 0

    lax.fori_loop(0, CHUNKS * blocks * BLOCK // 16, clear, 0)

    def clear_blocks(i, _):
        for k in range(16):
            order[page_base + i * 16 + k] = 0
        return 0

    lax.fori_loop(0, CHUNKS * blocks // 16, clear_blocks, 0)
    for i in range(CHUNKS * pages + 1):
        count[i] = 0

    def tally(s, _):
        for chunk in range(CHUNKS):
            for j in range(sub):
                code = arrived[s * capacity + chunk * sub + j]
                p = jnp.where(code < 0, CHUNKS * pages, (code & (pages - 1)) + chunk * pages)
                count[p] = count[p] + 1
        return 0

    lax.fori_loop(0, groups, tally, 0)

    for chunk in range(CHUNKS):

        def lay(p, b):
            n = count[chunk * pages + p]
            first[chunk * pages + p] = b * BLOCK
            count[chunk * pages + p] = 0
            steps = lax.shift_right_logical(n + BLOCK - 1, 2)

            def one(k, _):
                order[page_base + b + k] = p
                return 0

            lax.fori_loop(0, steps, one, 0)
            return b + steps

        total = lax.fori_loop(0, pages, lay, jnp.int32(chunk * blocks))
        order[total_base + chunk] = total - chunk * blocks
    first[CHUNKS * pages] = total_base + 8
    count[CHUNKS * pages] = 0

    def source(s, _):
        side = lax.shift_right_logical(s, 4)
        slot = side * STRIDE + (s & 15) * sub
        base = s * query_count + slot * 2048
        for chunk in range(CHUNKS):
            for j in range(sub):
                code = arrived[s * capacity + chunk * sub + j]
                p = jnp.where(code < 0, CHUNKS * pages, (code & (pages - 1)) + chunk * pages)
                q = lax.shift_right_logical(jnp.maximum(code, 0), page_bits)
                r = count[p]
                count[p] = r + 1
                order[first[p] + r] = q + base + j * 2048
        return 0

    lax.fori_loop(0, groups, source, 0)


def split(x):
    parts = []
    for _ in range(PIECES):
        part = x.astype(BF16)
        parts.append(part)
        x = x - part.astype(F32)
    return parts


def pair_kernel(chunk, blocks, scale, order, limits, me, *refs):
    page_base = CHUNKS * blocks * BLOCK
    total_base = page_base + CHUNKS * blocks
    pages, held = refs[:2]
    outs = refs[2:10]
    wide, stats = refs[10:]
    part = pages.shape[1]
    tokens = held.shape[1]
    share = tokens // 4
    power = scale * math.log2(math.e)
    lane = lax.broadcasted_iota(jnp.int32, (1, part), 1)
    lanes = lax.broadcasted_iota(jnp.int32, (tokens, LANES), 1)

    def step(it, _):
        for u in range(UNROLL):
            b = chunk * blocks + it * UNROLL + u
            p = order[page_base + b]
            codes = [order[b * BLOCK + i] for i in range(BLOCK)]
            block = jnp.concatenate([held[c & 2047] for c in codes], axis=0)
            page = pages[p]
            raw = lax.dot_general(block, page, (((1,), (1,)), ((), ())), preferred_element_type=F32)
            raw = jnp.where(lane < limits[p], raw, NEG)
            top = jnp.max(raw, axis=1, keepdims=True)
            weights = jnp.exp2((raw - top) * power)
            total = jnp.sum(weights, axis=1, keepdims=True)
            out = jnp.dot(weights.astype(BF16), page, preferred_element_type=F32)
            peak = jnp.maximum(top * scale, NEG)
            for i in range(BLOCK):
                slot = lax.shift_right_logical(codes[i], 11)
                for t in range(4):
                    first = i * tokens + t * share
                    wide[t, pl.ds(pl.multiple_of(slot * share, share), share), :] = out[first : first + share]
                here = lanes == (slot & (LANES - 1))
                at = lax.shift_right_logical(slot, 7)
                rows = slice(i * tokens, (i + 1) * tokens)
                stats[0, at] = jnp.where(here, peak[rows], stats[0, at])
                stats[1, at] = jnp.where(here, total[rows], stats[1, at])
        return 0

    lax.fori_loop(0, (order[total_base + chunk] + UNROLL - 1) // UNROLL, step, 0)

    rep = me[0]
    length = outs[0].shape[0] - 2 * PIECES * 2 * share
    piece = 512
    for p in range(4):
        t = (rep + p) & 3
        for h in range(2):
            out = outs[p * 2 + h]

            def narrow(i, _):
                at = pl.multiple_of(i * piece, piece)
                out[pl.ds(at, piece), :] = wide[t, pl.ds(at + h * STRIDE * share, piece), :].astype(BF16)
                return 0

            lax.fori_loop(0, length // piece, narrow, 0)
            for s in range(2):
                rows = pl.ds(pl.multiple_of(t * share, share), share)
                both = jnp.concatenate([stats[s, h * 2, rows, :], stats[s, h * 2 + 1, rows, :]], axis=0)
                for k, x in enumerate(split(both)):
                    at = length + (s * PIECES + k) * 2 * share
                    out[at : at + 2 * share, :] = x


def merge_kernel(last, root, share, sub, *refs):
    n_in = 4 * CHUNKS if last else 4
    ins = refs[:n_in]
    outs = refs[n_in:]
    length = ins[0].shape[0] - 2 * PIECES * 2 * share
    span = 2 * sub * share + 2 * share
    for n in range(n_in // 2):
        chunk, h = n // 2, n % 2
        came, own = ins[2 * n], ins[2 * n + 1]

        def joined(ref, s):
            at = length + s * PIECES * 2 * share
            tiles = [ref[at + k * 2 * share : at + (k + 1) * 2 * share, :].astype(F32) for k in range(PIECES)]
            return tiles[0] + (tiles[1] + tiles[2])

        peak_a, total_a, peak_b, total_b = joined(came, 0), joined(came, 1), joined(own, 0), joined(own, 1)
        peak = jnp.maximum(peak_a, peak_b)
        part_a, part_b = jnp.exp(peak_a - peak), jnp.exp(peak_b - peak)
        total = total_a * part_a + total_b * part_b
        if last:
            part_a, part_b = part_a / (total * root), part_b / (total * root)
            logs = TAU * (peak + jnp.log(total))
            rows = [jnp.sum(logs[k * share : (k + 1) * share], axis=0, keepdims=True) for k in range(2)]
            if chunk == 0:
                kept = {**(kept if h else {}), h: rows}
            else:
                both = jnp.concatenate(kept[h] + rows, axis=0)
                tile = jnp.concatenate([x.astype(F32) for x in split(both)] + [both * 0.0], axis=0).astype(BF16)
                sources = length // (sub * share)
                for source in range(sources):
                    at = (h * sources + source) * span + 2 * sub * share
                    outs[0][at : at + 2 * share, :] = tile
        else:
            for s, x in enumerate((peak, total)):
                for k, tile in enumerate(split(x)):
                    at = length + (s * PIECES + k) * 2 * share
                    outs[h][at : at + 2 * share, :] = tile
        for pair in range(length // (2 * share)):
            at = pair * 2 * share

            def factor(x):
                columns = []
                for slot in (2 * pair, 2 * pair + 1):
                    k, lane = slot // LANES, slot % LANES
                    columns.append(jnp.broadcast_to(x[k * share : (k + 1) * share, lane : lane + 1], (share, LANES)))
                return jnp.concatenate(columns, axis=0)

            rows = slice(at, at + 2 * share)
            value = came[rows, :].astype(F32) * factor(part_a) + own[rows, :].astype(F32) * factor(part_b)
            if last:
                source, j = 2 * pair // sub, 2 * pair % sub
                to = (h * (length // (sub * share)) + source) * span + (chunk * sub + j) * share
                outs[0][to : to + 2 * share, :] = value.astype(BF16)
            else:
                outs[h][rows, :] = value.astype(BF16)


def gradient_kernel(share, list_len, place, weight, directions, out, wide):
    def widen(i, _):
        at = pl.multiple_of(i * 128, 128)
        wide[pl.ds(at, 128), :] = directions[pl.ds(at, 128), :].astype(F32)
        return 0

    lax.fori_loop(0, directions.shape[0] // 128, widen, 0)

    def step(i, _):
        parts = []
        for s in range(2):
            total = jnp.zeros((share, out.shape[1]), F32)
            for k in range(list_len):
                e = (i * 2 + s) * list_len + k
                at = pl.multiple_of(place[e] * share, share)
                total = total + weight[e] * wide[pl.ds(at, share), :]
            parts.append(total)
        out[pl.ds(pl.multiple_of(i * 2 * share, 2 * share), 2 * share), :] = jnp.concatenate(parts, axis=0).astype(BF16)
        return 0

    lax.fori_loop(0, out.shape[0] // share // 2, step, 0)


def ints(*shape):
    return jax.ShapeDtypeStruct(shape, jnp.int32)


def per_device(queries, listed, page_slot, counts, page_store):
    groups = lax.axis_size("index")
    index = lax.axis_index("index").astype(jnp.int32)
    rep = lax.axis_index("rep").astype(jnp.int32)
    reps = lax.axis_size("rep")
    query_count, query_len, feature = queries.shape
    list_len = listed.shape[1]
    pages, part, _ = page_store.shape
    page_bits = pages.bit_length() - 1
    pairs = query_count * list_len
    capacity = 2 * pairs // groups
    sub = capacity // CHUNKS
    slots = groups * capacity
    share = query_len // reps
    blocks = (groups * sub + (BLOCK - 1) * pages) // BLOCK
    blocks = (blocks + UNROLL - 1) // UNROLL * UNROLL
    root = math.sqrt(feature)
    scale = 1.0 / (root * TAU)

    table, place, tile = pl.pallas_call(
        functools.partial(route_kernel, capacity, page_bits, list_len),
        out_shape=(ints(slots), ints(pairs), ints(pairs)),
        in_specs=[SMEM, SMEM],
        out_specs=(SMEM,) * 3,
        scratch_shapes=[pltpu.SMEM((groups,), jnp.int32)],
        name="route",
    )(listed.reshape(pairs), page_slot)
    arrived = lax.all_to_all(table.reshape(groups, capacity), "index", split_axis=0, concat_axis=0, tiled=True)

    everyone = lax.all_gather(queries, "index", tiled=True)

    order = pl.pallas_call(
        functools.partial(sort_kernel, capacity, page_bits, query_count, blocks),
        out_shape=ints(CHUNKS * blocks * (BLOCK + 1) + 8 + slots),
        in_specs=[SMEM],
        out_specs=SMEM,
        scratch_shapes=[pltpu.SMEM((CHUNKS * pages + 1,), jnp.int32)] * 2,
        cost_estimate=pl.CostEstimate(flops=0, bytes_accessed=40_000_000, transcendentals=0),
        name="sort_pairs",
    )(arrived.reshape(slots))

    limits = counts - rep * part
    me = rep[None]

    length = groups // 2 * sub * share
    packed = length + 2 * PIECES * 2 * share

    def rep_pairs(step):
        return [(i, (i + step) % reps) for i in range(reps)]

    def travel(x, step):
        return lax.ppermute(x, "rep", rep_pairs(step))

    finals = []
    for chunk in range(CHUNKS):
        parts = pl.pallas_call(
            functools.partial(pair_kernel, chunk, blocks, scale),
            out_shape=(jax.ShapeDtypeStruct((packed, feature), BF16),) * 8,
            in_specs=[SMEM] * 3 + [VMEM] * 2,
            out_specs=(VMEM,) * 8,
            scratch_shapes=[
                pltpu.VMEM((4, 2 * STRIDE * share, feature), F32),
                pltpu.VMEM((2, 2 * STRIDE // LANES, query_len, LANES), F32),
            ],
            compiler_params=params(28),
            cost_estimate=pl.CostEstimate(flops=0, bytes_accessed=60_000_000, transcendentals=0),
            name="pairs",
        )(order, limits, me, page_store, everyone)

        held = [parts[3 * 2], parts[1 * 2 + 1]]
        for hop in range(3):
            came = [travel(held[0], 1), travel(held[1], -1)]
            own = [parts[(2, 1, 0)[hop] * 2], parts[(2, 3, 0)[hop] * 2 + 1]]
            if hop == 2:
                finals += [came[0], own[0], came[1], own[1]]
                break
            held = pl.pallas_call(
                functools.partial(merge_kernel, False, root, share, sub),
                out_shape=(jax.ShapeDtypeStruct((packed, feature), BF16),) * 2,
                in_specs=[VMEM] * 4,
                out_specs=(VMEM,) * 2,
                compiler_params=params(24),
                cost_estimate=pl.CostEstimate(flops=0, bytes_accessed=8_000_000, transcendentals=0),
                name="merge",
            )(came[0], own[0], came[1], own[1])
    span = 2 * sub * share + 2 * share
    outgoing = pl.pallas_call(
        functools.partial(merge_kernel, True, root, share, sub),
        out_shape=jax.ShapeDtypeStruct((groups * span, feature), BF16),
        in_specs=[VMEM] * (4 * CHUNKS),
        out_specs=VMEM,
        compiler_params=params(24),
        name="merge_last",
    )(*finals)
    returned = lax.all_to_all(outgoing.reshape(groups, span, feature), "index", split_axis=0, concat_axis=0, tiled=True)

    logs = returned[:, capacity * share : capacity * share + 4 * PIECES].astype(F32)
    logs = jnp.sum(logs.reshape(groups, PIECES, CHUNKS, STRIDE), axis=1)
    logs = lax.dynamic_slice_in_dim(logs, (index % (groups // 2)) * sub, sub, 2).reshape(slots)
    logs = logs + travel(logs, 1) + travel(logs, -1) + travel(logs, 2)
    pair_scores = logs[place].reshape(query_count, list_len)
    highest = jnp.max(pair_scores, axis=1, keepdims=True)
    log_total = highest[:, 0] + jnp.log(jnp.sum(jnp.exp(pair_scores - highest), axis=1))
    losses = log_total - pair_scores[:, 0]
    probability = jnp.exp(pair_scores - log_total[:, None])
    target = (jnp.arange(list_len) == 0).astype(F32)
    coefficient = LOSS_SCALE * (probability - target[None, :])

    quarter = pl.pallas_call(
        functools.partial(gradient_kernel, share, list_len),
        out_shape=jax.ShapeDtypeStruct((query_count * share, feature), BF16),
        in_specs=[SMEM, SMEM, VMEM],
        out_specs=VMEM,
        scratch_shapes=[pltpu.VMEM((groups * span, feature), F32)],
        compiler_params=params(32),
        name="gradients",
    )(tile, coefficient.reshape(pairs), returned.reshape(groups * span, feature))
    gathered = lax.all_gather(quarter.reshape(query_count, share, feature), "rep")
    gradients = jnp.transpose(gathered, (1, 0, 2, 3)).reshape(query_count, query_len, feature)
    return (losses, gradients)


def solution(mesh):
    return jax.shard_map(
        per_device,
        mesh=mesh,
        in_specs=(
            P("index", None, None),
            P("index", None),
            P(),
            P("index"),
            P("index", "rep", None),
        ),
        out_specs=(P("index"), P("index", None, None)),
        check_vma=False,
    )
```

```python
import functools
import math

import jax
import jax.numpy as jnp
from jax import lax
from jax.experimental import pallas as pl
from jax.experimental.pallas import tpu as pltpu
from jax.sharding import PartitionSpec as P

TAU = 0.1
LOSS_SCALE = 32.0
NEG = -1e30
BLOCK = 4
UNROLL = 32
CHUNKS = 2
LANES = 128
STRIDE = 256
PIECES = 3
F32 = jnp.float32
BF16 = jnp.bfloat16

SMEM = pl.BlockSpec(memory_space=pltpu.SMEM)
VMEM = pl.BlockSpec(memory_space=pltpu.VMEM)
ANY = pl.BlockSpec(memory_space=pl.ANY)


def params(mib):
    return pltpu.CompilerParams(vmem_limit_bytes=mib * 1024 * 1024)


def route_kernel(capacity, page_bits, list_len, listed, page_slot, table, place, tile, used):
    slots = table.shape[0]
    pairs = listed.shape[0]
    groups = used.shape[0]
    sub = capacity // CHUNKS

    def clear(i, _):
        for k in range(16):
            table[i * 16 + k] = -1
        return 0

    lax.fori_loop(0, slots // 16, clear, 0)
    for i in range(groups):
        used[i] = 0

    def step(q, _):
        for k in range(list_len):
            i = q * list_len + k
            row = page_slot[listed[i]]
            owner = lax.shift_right_logical(row, page_bits)
            n = jnp.minimum(used[owner], capacity - 1)
            used[owner] = n + 1
            chunk = n & 1
            j = lax.shift_right_logical(n, 1)
            table[owner * capacity + chunk * sub + j] = lax.shift_left(q, page_bits) + (row & ((1 << page_bits) - 1))
            place[i] = owner * capacity + chunk * sub + j
            tile[i] = owner * (capacity + 2) + chunk * sub + j
        return 0

    lax.fori_loop(0, pairs // list_len, step, 0)


def sort_kernel(capacity, page_bits, query_count, blocks, arrived, order, count, first):
    page_base = CHUNKS * blocks * BLOCK
    total_base = page_base + CHUNKS * blocks
    slots = arrived.shape[0]
    groups = slots // capacity
    sub = capacity // CHUNKS
    pages = 1 << page_bits
    nothing = (groups // 2) * sub * 2048

    def clear(i, _):
        for k in range(16):
            order[i * 16 + k] = nothing
        return 0

    lax.fori_loop(0, CHUNKS * blocks * BLOCK // 16, clear, 0)

    def clear_blocks(i, _):
        for k in range(16):
            order[page_base + i * 16 + k] = 0
        return 0

    lax.fori_loop(0, CHUNKS * blocks // 16, clear_blocks, 0)
    for i in range(CHUNKS * pages + 1):
        count[i] = 0

    def tally(s, _):
        for chunk in range(CHUNKS):
            for j in range(sub):
                code = arrived[s * capacity + chunk * sub + j]
                p = jnp.where(code < 0, CHUNKS * pages, (code & (pages - 1)) + chunk * pages)
                count[p] = count[p] + 1
        return 0

    lax.fori_loop(0, groups, tally, 0)

    for chunk in range(CHUNKS):

        def lay(p, b):
            n = count[chunk * pages + p]
            first[chunk * pages + p] = b * BLOCK
            count[chunk * pages + p] = 0
            steps = lax.shift_right_logical(n + BLOCK - 1, 2)

            def one(k, _):
                order[page_base + b + k] = p
                return 0

            lax.fori_loop(0, steps, one, 0)
            return b + steps

        total = lax.fori_loop(0, pages, lay, jnp.int32(chunk * blocks))
        order[total_base + chunk] = total - chunk * blocks
    first[CHUNKS * pages] = total_base + 8
    count[CHUNKS * pages] = 0

    def source(s, _):
        side = lax.shift_right_logical(s, 4)
        slot = side * STRIDE + (s & 15) * sub
        base = s * query_count + slot * 2048
        for chunk in range(CHUNKS):
            for j in range(sub):
                code = arrived[s * capacity + chunk * sub + j]
                p = jnp.where(code < 0, CHUNKS * pages, (code & (pages - 1)) + chunk * pages)
                q = lax.shift_right_logical(jnp.maximum(code, 0), page_bits)
                r = count[p]
                count[p] = r + 1
                order[first[p] + r] = q + base + j * 2048
        return 0

    lax.fori_loop(0, groups, source, 0)


def split(x):
    parts = []
    for _ in range(PIECES):
        part = x.astype(BF16)
        parts.append(part)
        x = x - part.astype(F32)
    return parts


def pair_kernel(chunk, blocks, scale, order, limits, me, *refs):
    page_base = CHUNKS * blocks * BLOCK
    total_base = page_base + CHUNKS * blocks
    pages, held = refs[:2]
    outs = refs[2:10]
    wide, stats = refs[10:12]
    if chunk == 0:
        copies = [pltpu.make_async_copy(x, y, refs[14].at[k]) for k, (x, y) in enumerate(zip(refs[:2], refs[12:14], strict=True))]
        for c in copies:
            c.start()
        for c in copies:
            c.wait()
        pages, held = refs[12:14]
    part = pages.shape[1]
    tokens = held.shape[1]
    share = tokens // 4
    power = scale * math.log2(math.e)
    lane = lax.broadcasted_iota(jnp.int32, (1, part), 1)
    lanes = lax.broadcasted_iota(jnp.int32, (tokens, LANES), 1)

    def step(it, _):
        for u in range(UNROLL):
            b = chunk * blocks + it * UNROLL + u
            p = order[page_base + b]
            codes = [order[b * BLOCK + i] for i in range(BLOCK)]
            block = jnp.concatenate([held[c & 2047] for c in codes], axis=0)
            page = pages[p]
            raw = lax.dot_general(block, page, (((1,), (1,)), ((), ())), preferred_element_type=F32)
            raw = jnp.where(lane < limits[p], raw, NEG)
            top = jnp.max(raw, axis=1, keepdims=True)
            weights = jnp.exp2((raw - top) * power)
            total = jnp.sum(weights, axis=1, keepdims=True)
            out = jnp.dot(weights.astype(BF16), page, preferred_element_type=F32)
            peak = jnp.maximum(top * scale, NEG)
            for i in range(BLOCK):
                slot = lax.shift_right_logical(codes[i], 11)
                for t in range(4):
                    first = i * tokens + t * share
                    wide[t, pl.ds(pl.multiple_of(slot * share, share), share), :] = out[first : first + share]
                here = lanes == (slot & (LANES - 1))
                at = lax.shift_right_logical(slot, 7)
                rows = slice(i * tokens, (i + 1) * tokens)
                stats[0, at] = jnp.where(here, peak[rows], stats[0, at])
                stats[1, at] = jnp.where(here, total[rows], stats[1, at])
        return 0

    lax.fori_loop(0, (order[total_base + chunk] + UNROLL - 1) // UNROLL, step, 0)

    rep = me[0]
    length = outs[0].shape[0] - 2 * PIECES * 2 * share
    piece = 512
    for p in range(4):
        t = (rep + p) & 3
        for h in range(2):
            out = outs[p * 2 + h]

            def narrow(i, _):
                at = pl.multiple_of(i * piece, piece)
                out[pl.ds(at, piece), :] = wide[t, pl.ds(at + h * STRIDE * share, piece), :].astype(BF16)
                return 0

            lax.fori_loop(0, length // piece, narrow, 0)
            for s in range(2):
                rows = pl.ds(pl.multiple_of(t * share, share), share)
                both = jnp.concatenate([stats[s, h * 2, rows, :], stats[s, h * 2 + 1, rows, :]], axis=0)
                for k, x in enumerate(split(both)):
                    at = length + (s * PIECES + k) * 2 * share
                    out[at : at + 2 * share, :] = x


def merge_kernel(last, root, share, sub, *refs):
    n_in = 4 * CHUNKS if last else 4
    ins = refs[:n_in]
    outs = refs[n_in:]
    length = ins[0].shape[0] - 2 * PIECES * 2 * share
    span = 2 * sub * share + 2 * share
    for n in range(n_in // 2):
        chunk, h = n // 2, n % 2
        came, own = ins[2 * n], ins[2 * n + 1]

        def joined(ref, s):
            at = length + s * PIECES * 2 * share
            tiles = [ref[at + k * 2 * share : at + (k + 1) * 2 * share, :].astype(F32) for k in range(PIECES)]
            return tiles[0] + (tiles[1] + tiles[2])

        peak_a, total_a, peak_b, total_b = joined(came, 0), joined(came, 1), joined(own, 0), joined(own, 1)
        peak = jnp.maximum(peak_a, peak_b)
        part_a, part_b = jnp.exp(peak_a - peak), jnp.exp(peak_b - peak)
        total = total_a * part_a + total_b * part_b
        if last:
            part_a, part_b = part_a / (total * root), part_b / (total * root)
            logs = TAU * (peak + jnp.log(total))
            rows = [jnp.sum(logs[k * share : (k + 1) * share], axis=0, keepdims=True) for k in range(2)]
            if chunk == 0:
                kept = {**(kept if h else {}), h: rows}
            else:
                both = jnp.concatenate(kept[h] + rows, axis=0)
                tile = jnp.concatenate([x.astype(F32) for x in split(both)] + [both * 0.0], axis=0).astype(BF16)
                sources = length // (sub * share)
                for source in range(sources):
                    at = (h * sources + source) * span + 2 * sub * share
                    outs[0][at : at + 2 * share, :] = tile
        else:
            for s, x in enumerate((peak, total)):
                for k, tile in enumerate(split(x)):
                    at = length + (s * PIECES + k) * 2 * share
                    outs[h][at : at + 2 * share, :] = tile
        for pair in range(length // (2 * share)):
            at = pair * 2 * share

            def factor(x):
                columns = []
                for slot in (2 * pair, 2 * pair + 1):
                    k, lane = slot // LANES, slot % LANES
                    columns.append(jnp.broadcast_to(x[k * share : (k + 1) * share, lane : lane + 1], (share, LANES)))
                return jnp.concatenate(columns, axis=0)

            rows = slice(at, at + 2 * share)
            value = came[rows, :].astype(F32) * factor(part_a) + own[rows, :].astype(F32) * factor(part_b)
            if last:
                source, j = 2 * pair // sub, 2 * pair % sub
                to = (h * (length // (sub * share)) + source) * span + (chunk * sub + j) * share
                outs[0][to : to + 2 * share, :] = value.astype(BF16)
            else:
                outs[h][rows, :] = value.astype(BF16)


def gradient_kernel(share, list_len, place, weight, directions, out, wide):
    def widen(i, _):
        at = pl.multiple_of(i * 128, 128)
        wide[pl.ds(at, 128), :] = directions[pl.ds(at, 128), :].astype(F32)
        return 0

    lax.fori_loop(0, directions.shape[0] // 128, widen, 0)

    def step(i, _):
        parts = []
        for s in range(2):
            total = jnp.zeros((share, out.shape[1]), F32)
            for k in range(list_len):
                e = (i * 2 + s) * list_len + k
                at = pl.multiple_of(place[e] * share, share)
                total = total + weight[e] * wide[pl.ds(at, share), :]
            parts.append(total)
        out[pl.ds(pl.multiple_of(i * 2 * share, 2 * share), 2 * share), :] = jnp.concatenate(parts, axis=0).astype(BF16)
        return 0

    lax.fori_loop(0, out.shape[0] // share // 2, step, 0)


def ints(*shape):
    return jax.ShapeDtypeStruct(shape, jnp.int32)


def per_device(queries, listed, page_slot, counts, page_store):
    groups = lax.axis_size("index")
    index = lax.axis_index("index").astype(jnp.int32)
    rep = lax.axis_index("rep").astype(jnp.int32)
    reps = lax.axis_size("rep")
    query_count, query_len, feature = queries.shape
    list_len = listed.shape[1]
    pages, part, _ = page_store.shape
    page_bits = pages.bit_length() - 1
    pairs = query_count * list_len
    capacity = 2 * pairs // groups
    sub = capacity // CHUNKS
    slots = groups * capacity
    share = query_len // reps
    blocks = (groups * sub + (BLOCK - 1) * pages) // BLOCK
    blocks = (blocks + UNROLL - 1) // UNROLL * UNROLL
    root = math.sqrt(feature)
    scale = 1.0 / (root * TAU)

    table, place, tile = pl.pallas_call(
        functools.partial(route_kernel, capacity, page_bits, list_len),
        out_shape=(ints(slots), ints(pairs), ints(pairs)),
        in_specs=[SMEM, SMEM],
        out_specs=(SMEM,) * 3,
        scratch_shapes=[pltpu.SMEM((groups,), jnp.int32)],
        name="route",
    )(listed.reshape(pairs), page_slot)
    arrived = lax.all_to_all(table.reshape(groups, capacity), "index", split_axis=0, concat_axis=0, tiled=True)

    everyone = lax.all_gather(queries, "index", tiled=True)

    order = pl.pallas_call(
        functools.partial(sort_kernel, capacity, page_bits, query_count, blocks),
        out_shape=ints(CHUNKS * blocks * (BLOCK + 1) + 8 + slots),
        in_specs=[SMEM],
        out_specs=SMEM,
        scratch_shapes=[pltpu.SMEM((CHUNKS * pages + 1,), jnp.int32)] * 2,
        cost_estimate=pl.CostEstimate(flops=0, bytes_accessed=40_000_000, transcendentals=0),
        name="sort_pairs",
    )(arrived.reshape(slots))

    limits = counts - rep * part
    me = rep[None]

    length = groups // 2 * sub * share
    packed = length + 2 * PIECES * 2 * share

    def rep_pairs(step):
        return [(i, (i + step) % reps) for i in range(reps)]

    def travel(x, step):
        return lax.ppermute(x, "rep", rep_pairs(step))

    finals = []
    for chunk in range(CHUNKS):
        parts = pl.pallas_call(
            functools.partial(pair_kernel, chunk, blocks, scale),
            out_shape=(jax.ShapeDtypeStruct((packed, feature), BF16),) * 8,
            in_specs=[SMEM] * 3 + [VMEM if chunk else ANY] * 2,
            out_specs=(VMEM,) * 8,
            scratch_shapes=[
                pltpu.VMEM((4, 2 * STRIDE * share, feature), F32),
                pltpu.VMEM((2, 2 * STRIDE // LANES, query_len, LANES), F32),
            ]
            + ([] if chunk else [pltpu.VMEM(x.shape, BF16) for x in (page_store, everyone)] + [pltpu.SemaphoreType.DMA((2,))]),
            compiler_params=params(28 if chunk else 36),
            cost_estimate=pl.CostEstimate(flops=0, bytes_accessed=60_000_000, transcendentals=0),
            name="pairs",
        )(order, limits, me, page_store, everyone)

        held = [parts[3 * 2], parts[1 * 2 + 1]]
        for hop in range(3):
            came = [travel(held[0], 1), travel(held[1], -1)]
            own = [parts[(2, 1, 0)[hop] * 2], parts[(2, 3, 0)[hop] * 2 + 1]]
            if hop == 2:
                finals += [came[0], own[0], came[1], own[1]]
                break
            held = pl.pallas_call(
                functools.partial(merge_kernel, False, root, share, sub),
                out_shape=(jax.ShapeDtypeStruct((packed, feature), BF16),) * 2,
                in_specs=[VMEM] * 4,
                out_specs=(VMEM,) * 2,
                compiler_params=params(24),
                cost_estimate=pl.CostEstimate(flops=0, bytes_accessed=8_000_000, transcendentals=0),
                name="merge",
            )(came[0], own[0], came[1], own[1])
    span = 2 * sub * share + 2 * share
    outgoing = pl.pallas_call(
        functools.partial(merge_kernel, True, root, share, sub),
        out_shape=jax.ShapeDtypeStruct((groups * span, feature), BF16),
        in_specs=[VMEM] * (4 * CHUNKS),
        out_specs=VMEM,
        compiler_params=params(24),
        name="merge_last",
    )(*finals)
    returned = lax.all_to_all(outgoing.reshape(groups, span, feature), "index", split_axis=0, concat_axis=0, tiled=True)

    logs = returned[:, capacity * share : capacity * share + 4 * PIECES].astype(F32)
    logs = jnp.sum(logs.reshape(groups, PIECES, CHUNKS, STRIDE), axis=1)
    logs = lax.dynamic_slice_in_dim(logs, (index % (groups // 2)) * sub, sub, 2).reshape(slots)
    logs = logs + travel(logs, 1) + travel(logs, -1) + travel(logs, 2)
    pair_scores = logs[place].reshape(query_count, list_len)
    highest = jnp.max(pair_scores, axis=1, keepdims=True)
    log_total = highest[:, 0] + jnp.log(jnp.sum(jnp.exp(pair_scores - highest), axis=1))
    losses = log_total - pair_scores[:, 0]
    probability = jnp.exp(pair_scores - log_total[:, None])
    target = (jnp.arange(list_len) == 0).astype(F32)
    coefficient = LOSS_SCALE * (probability - target[None, :])

    quarter = pl.pallas_call(
        functools.partial(gradient_kernel, share, list_len),
        out_shape=jax.ShapeDtypeStruct((query_count * share, feature), BF16),
        in_specs=[SMEM, SMEM, VMEM],
        out_specs=VMEM,
        scratch_shapes=[pltpu.VMEM((groups * span, feature), F32)],
        compiler_params=params(32),
        name="gradients",
    )(tile, coefficient.reshape(pairs), returned.reshape(groups * span, feature))
    gathered = lax.all_gather(quarter.reshape(query_count, share, feature), "rep")
    gradients = jnp.transpose(gathered, (1, 0, 2, 3)).reshape(query_count, query_len, feature)
    return (losses, gradients)


def solution(mesh):
    return jax.shard_map(
        per_device,
        mesh=mesh,
        in_specs=(
            P("index", None, None),
            P("index", None),
            P(),
            P("index"),
            P("index", "rep", None),
        ),
        out_specs=(P("index"), P("index", None, None)),
        check_vma=False,
    )
```

```python
import functools
import math

import jax
import jax.numpy as jnp
from jax import lax
from jax.experimental import pallas as pl
from jax.experimental.pallas import tpu as pltpu
from jax.sharding import PartitionSpec as P

TAU = 0.1
LOSS_SCALE = 32.0
NEG = -1e30
BLOCK = 4
UNROLL = 16
CHUNKS = 2
LANES = 128
STRIDE = 256
PIECES = 3
F32 = jnp.float32
BF16 = jnp.bfloat16

SMEM = pl.BlockSpec(memory_space=pltpu.SMEM)
VMEM = pl.BlockSpec(memory_space=pltpu.VMEM)
ANY = pl.BlockSpec(memory_space=pl.ANY)


def params(mib):
    return pltpu.CompilerParams(vmem_limit_bytes=mib * 1024 * 1024)


def route_kernel(capacity, page_bits, list_len, listed, page_slot, table, place, tile, used):
    slots = table.shape[0]
    pairs = listed.shape[0]
    groups = used.shape[0]
    sub = capacity // CHUNKS

    def clear(i, _):
        for k in range(16):
            table[i * 16 + k] = -1
        return 0

    lax.fori_loop(0, slots // 16, clear, 0)
    for i in range(groups):
        used[i] = 0

    def step(q, _):
        for k in range(list_len):
            i = q * list_len + k
            row = page_slot[listed[i]]
            owner = lax.shift_right_logical(row, page_bits)
            n = jnp.minimum(used[owner], capacity - 1)
            used[owner] = n + 1
            chunk = n & 1
            j = lax.shift_right_logical(n, 1)
            table[owner * capacity + chunk * sub + j] = lax.shift_left(q, page_bits) + (row & ((1 << page_bits) - 1))
            place[i] = owner * capacity + chunk * sub + j
            tile[i] = owner * (capacity + 2) + chunk * sub + j
        return 0

    lax.fori_loop(0, pairs // list_len, step, 0)


def sort_kernel(capacity, page_bits, query_count, blocks, arrived, order, count, first):
    page_base = CHUNKS * blocks * BLOCK
    total_base = page_base + CHUNKS * blocks
    slots = arrived.shape[0]
    groups = slots // capacity
    sub = capacity // CHUNKS
    pages = 1 << page_bits
    nothing = (groups // 2) * sub * 2048

    def clear(i, _):
        for k in range(16):
            order[i * 16 + k] = nothing
        return 0

    lax.fori_loop(0, CHUNKS * blocks * BLOCK // 16, clear, 0)

    def clear_blocks(i, _):
        for k in range(16):
            order[page_base + i * 16 + k] = 0
        return 0

    lax.fori_loop(0, CHUNKS * blocks // 16, clear_blocks, 0)
    for i in range(CHUNKS * pages + 1):
        count[i] = 0

    def tally(s, _):
        for chunk in range(CHUNKS):
            for j in range(sub):
                code = arrived[s * capacity + chunk * sub + j]
                p = jnp.where(code < 0, CHUNKS * pages, (code & (pages - 1)) + chunk * pages)
                count[p] = count[p] + 1
        return 0

    lax.fori_loop(0, groups, tally, 0)

    for chunk in range(CHUNKS):

        def lay(p, b):
            n = count[chunk * pages + p]
            first[chunk * pages + p] = b * BLOCK
            count[chunk * pages + p] = 0
            steps = lax.shift_right_logical(n + BLOCK - 1, 2)

            def one(k, _):
                order[page_base + b + k] = p
                return 0

            lax.fori_loop(0, steps, one, 0)
            return b + steps

        total = lax.fori_loop(0, pages, lay, jnp.int32(chunk * blocks))
        order[total_base + chunk] = total - chunk * blocks
    first[CHUNKS * pages] = total_base + 8
    count[CHUNKS * pages] = 0

    def source(s, _):
        side = lax.shift_right_logical(s, 4)
        slot = side * STRIDE + (s & 15) * sub
        base = s * query_count + slot * 2048
        for chunk in range(CHUNKS):
            for j in range(sub):
                code = arrived[s * capacity + chunk * sub + j]
                p = jnp.where(code < 0, CHUNKS * pages, (code & (pages - 1)) + chunk * pages)
                q = lax.shift_right_logical(jnp.maximum(code, 0), page_bits)
                r = count[p]
                count[p] = r + 1
                order[first[p] + r] = q + base + j * 2048
        return 0

    lax.fori_loop(0, groups, source, 0)


def split(x):
    parts = []
    for _ in range(PIECES):
        part = x.astype(BF16)
        parts.append(part)
        x = x - part.astype(F32)
    return parts


def pair_kernel(chunk, blocks, scale, order, limits, me, *refs):
    page_base = CHUNKS * blocks * BLOCK
    total_base = page_base + CHUNKS * blocks
    pages, held = refs[:2]
    outs = refs[2:10]
    wide, stats = refs[10:]
    part = pages.shape[1]
    tokens = held.shape[1]
    share = tokens // 4
    power = scale * math.log2(math.e)
    lane = lax.broadcasted_iota(jnp.int32, (1, part), 1)
    lanes = lax.broadcasted_iota(jnp.int32, (tokens, LANES), 1)

    def step(it, _):
        for u in range(UNROLL):
            b = chunk * blocks + it * UNROLL + u
            p = order[page_base + b]
            codes = [order[b * BLOCK + i] for i in range(BLOCK)]
            block = jnp.concatenate([held[c & 2047] for c in codes], axis=0)
            page = pages[p]
            raw = lax.dot_general(block, page, (((1,), (1,)), ((), ())), preferred_element_type=F32)
            raw = jnp.where(lane < limits[p], raw, NEG)
            top = jnp.max(raw, axis=1, keepdims=True)
            weights = jnp.exp2((raw - top) * power)
            total = jnp.sum(weights, axis=1, keepdims=True)
            out = jnp.dot(weights.astype(BF16), page, preferred_element_type=F32)
            peak = jnp.maximum(top * scale, NEG)
            for i in range(BLOCK):
                slot = lax.shift_right_logical(codes[i], 11)
                for t in range(4):
                    first = i * tokens + t * share
                    wide[t, pl.ds(pl.multiple_of(slot * share, share), share), :] = out[first : first + share]
                here = lanes == (slot & (LANES - 1))
                at = lax.shift_right_logical(slot, 7)
                rows = slice(i * tokens, (i + 1) * tokens)
                stats[0, at] = jnp.where(here, peak[rows], stats[0, at])
                stats[1, at] = jnp.where(here, total[rows], stats[1, at])
        return 0

    lax.fori_loop(0, (order[total_base + chunk] + UNROLL - 1) // UNROLL, step, 0)

    rep = me[0]
    length = outs[0].shape[0] - 2 * PIECES * 2 * share
    piece = 512
    for p in range(4):
        t = (rep + p) & 3
        for h in range(2):
            out = outs[p * 2 + h]

            def narrow(i, _):
                at = pl.multiple_of(i * piece, piece)
                out[pl.ds(at, piece), :] = wide[t, pl.ds(at + h * STRIDE * share, piece), :].astype(BF16)
                return 0

            lax.fori_loop(0, length // piece, narrow, 0)
            for s in range(2):
                rows = pl.ds(pl.multiple_of(t * share, share), share)
                both = jnp.concatenate([stats[s, h * 2, rows, :], stats[s, h * 2 + 1, rows, :]], axis=0)
                for k, x in enumerate(split(both)):
                    at = length + (s * PIECES + k) * 2 * share
                    out[at : at + 2 * share, :] = x


def merge_kernel(last, root, share, sub, *refs):
    n_in = 4
    ins = refs[:n_in]
    outs = refs[-1:] if last == 2 else refs[n_in:]
    length = ins[0].shape[0] - 2 * PIECES * 2 * share
    span = 2 * sub * share + 2 * share
    for n in range(n_in // 2):
        chunk, h = max(last - 1, 0), n % 2
        came, own = ins[2 * n], ins[2 * n + 1]

        def joined(ref, s):
            at = length + s * PIECES * 2 * share
            tiles = [ref[at + k * 2 * share : at + (k + 1) * 2 * share, :].astype(F32) for k in range(PIECES)]
            return tiles[0] + (tiles[1] + tiles[2])

        peak_a, total_a, peak_b, total_b = joined(came, 0), joined(came, 1), joined(own, 0), joined(own, 1)
        peak = jnp.maximum(peak_a, peak_b)
        part_a, part_b = jnp.exp(peak_a - peak), jnp.exp(peak_b - peak)
        total = total_a * part_a + total_b * part_b
        if last:
            part_a, part_b = part_a / (total * root), part_b / (total * root)
            logs = TAU * (peak + jnp.log(total))
            rows = [jnp.sum(logs[k * share : (k + 1) * share], axis=0, keepdims=True) for k in range(2)]
            if chunk == 0:
                outs[1][2 * h : 2 * h + 2, :] = jnp.concatenate(rows, axis=0)
            else:
                both = jnp.concatenate([refs[n_in + 1][2 * h : 2 * h + 2, :]] + rows, axis=0)
                tile = jnp.concatenate([x.astype(F32) for x in split(both)] + [both * 0.0], axis=0).astype(BF16)
                sources = length // (sub * share)
                for source in range(sources):
                    at = (h * sources + source) * span + 2 * sub * share
                    outs[0][at : at + 2 * share, :] = tile
        else:
            for s, x in enumerate((peak, total)):
                for k, tile in enumerate(split(x)):
                    at = length + (s * PIECES + k) * 2 * share
                    outs[h][at : at + 2 * share, :] = tile
        for pair in range(length // (2 * share)):
            at = pair * 2 * share

            def factor(x):
                columns = []
                for slot in (2 * pair, 2 * pair + 1):
                    k, lane = slot // LANES, slot % LANES
                    columns.append(jnp.broadcast_to(x[k * share : (k + 1) * share, lane : lane + 1], (share, LANES)))
                return jnp.concatenate(columns, axis=0)

            rows = slice(at, at + 2 * share)
            value = came[rows, :].astype(F32) * factor(part_a) + own[rows, :].astype(F32) * factor(part_b)
            if last == 1:
                outs[0][h * length + pair * 2 * share : h * length + (pair + 1) * 2 * share, :] = value.astype(BF16)
            elif last:
                source, j = 2 * pair // sub, 2 * pair % sub
                to = (h * (length // (sub * share)) + source) * span + (chunk * sub + j) * share
                outs[0][to : to + 2 * share, :] = value.astype(BF16)
                earlier = h * length + pair * 2 * share
                to = to - sub * share
                outs[0][to : to + 2 * share, :] = refs[n_in][earlier : earlier + 2 * share, :]
            else:
                outs[h][rows, :] = value.astype(BF16)


def gradient_kernel(share, list_len, place, weight, directions, out, wide):
    def widen(i, _):
        at = pl.multiple_of(i * 128, 128)
        wide[pl.ds(at, 128), :] = directions[pl.ds(at, 128), :].astype(F32)
        return 0

    lax.fori_loop(0, directions.shape[0] // 128, widen, 0)

    def step(i, _):
        parts = []
        for s in range(2):
            total = jnp.zeros((share, out.shape[1]), F32)
            for k in range(list_len):
                e = (i * 2 + s) * list_len + k
                at = pl.multiple_of(place[e] * share, share)
                total = total + weight[e] * wide[pl.ds(at, share), :]
            parts.append(total)
        out[pl.ds(pl.multiple_of(i * 2 * share, 2 * share), 2 * share), :] = jnp.concatenate(parts, axis=0).astype(BF16)
        return 0

    lax.fori_loop(0, out.shape[0] // share // 2, step, 0)


def ints(*shape):
    return jax.ShapeDtypeStruct(shape, jnp.int32)


def per_device(queries, listed, page_slot, counts, page_store):
    groups = lax.axis_size("index")
    index = lax.axis_index("index").astype(jnp.int32)
    rep = lax.axis_index("rep").astype(jnp.int32)
    reps = lax.axis_size("rep")
    query_count, query_len, feature = queries.shape
    list_len = listed.shape[1]
    pages, part, _ = page_store.shape
    page_bits = pages.bit_length() - 1
    pairs = query_count * list_len
    capacity = 2 * pairs // groups
    sub = capacity // CHUNKS
    slots = groups * capacity
    share = query_len // reps
    blocks = (groups * sub + (BLOCK - 1) * pages) // BLOCK
    blocks = (blocks + UNROLL - 1) // UNROLL * UNROLL
    root = math.sqrt(feature)
    scale = 1.0 / (root * TAU)

    table, place, tile = pl.pallas_call(
        functools.partial(route_kernel, capacity, page_bits, list_len),
        out_shape=(ints(slots), ints(pairs), ints(pairs)),
        in_specs=[SMEM, SMEM],
        out_specs=(SMEM,) * 3,
        scratch_shapes=[pltpu.SMEM((groups,), jnp.int32)],
        name="route",
    )(listed.reshape(pairs), page_slot)
    arrived = lax.all_to_all(table.reshape(groups, capacity), "index", split_axis=0, concat_axis=0, tiled=True)

    everyone = lax.all_gather(queries, "index", tiled=True)

    order = pl.pallas_call(
        functools.partial(sort_kernel, capacity, page_bits, query_count, blocks),
        out_shape=ints(CHUNKS * blocks * (BLOCK + 1) + 8 + slots),
        in_specs=[SMEM],
        out_specs=SMEM,
        scratch_shapes=[pltpu.SMEM((CHUNKS * pages + 1,), jnp.int32)] * 2,
        cost_estimate=pl.CostEstimate(flops=0, bytes_accessed=40_000_000, transcendentals=0),
        name="sort_pairs",
    )(arrived.reshape(slots))

    limits = counts - rep * part
    me = rep[None]

    length = groups // 2 * sub * share
    packed = length + 2 * PIECES * 2 * share

    def rep_pairs(step):
        return [(i, (i + step) % reps) for i in range(reps)]

    def travel(x, step):
        return lax.ppermute(x, "rep", rep_pairs(step))

    finals = []
    for chunk in range(CHUNKS):
        parts = pl.pallas_call(
            functools.partial(pair_kernel, chunk, blocks, scale),
            out_shape=(jax.ShapeDtypeStruct((packed, feature), BF16),) * 8,
            in_specs=[SMEM] * 3 + [VMEM] * 2,
            out_specs=(VMEM,) * 8,
            scratch_shapes=[
                pltpu.VMEM((4, 2 * STRIDE * share, feature), F32),
                pltpu.VMEM((2, 2 * STRIDE // LANES, query_len, LANES), F32),
            ],
            compiler_params=params(28),
            cost_estimate=pl.CostEstimate(flops=0, bytes_accessed=60_000_000, transcendentals=0),
            name="pairs",
        )(order, limits, me, page_store, everyone)

        held = [parts[3 * 2], parts[1 * 2 + 1]]
        for hop in range(3):
            came = [travel(held[0], 1), travel(held[1], -1)]
            own = [parts[(2, 1, 0)[hop] * 2], parts[(2, 3, 0)[hop] * 2 + 1]]
            if hop == 2:
                finals = [came[0], own[0], came[1], own[1], *finals]
                if chunk == 0:
                    finals = pl.pallas_call(
                        functools.partial(merge_kernel, 1, root, share, sub),
                        out_shape=(jax.ShapeDtypeStruct((2 * length, feature), BF16), jax.ShapeDtypeStruct((4, LANES), F32)),
                        in_specs=[VMEM] * 4,
                        out_specs=(VMEM,) * 2,
                        compiler_params=params(24),
                        cost_estimate=pl.CostEstimate(flops=0, bytes_accessed=8_000_000, transcendentals=0),
                        name="merge_first",
                    )(*finals)
                break
            held = pl.pallas_call(
                functools.partial(merge_kernel, 0, root, share, sub),
                out_shape=(jax.ShapeDtypeStruct((packed, feature), BF16),) * 2,
                in_specs=[VMEM] * 4,
                out_specs=(VMEM,) * 2,
                compiler_params=params(24),
                cost_estimate=pl.CostEstimate(flops=0, bytes_accessed=8_000_000, transcendentals=0),
                name="merge",
            )(came[0], own[0], came[1], own[1])
    span = 2 * sub * share + 2 * share
    outgoing = pl.pallas_call(
        functools.partial(merge_kernel, 2, root, share, sub),
        out_shape=jax.ShapeDtypeStruct((groups * span, feature), BF16),
        in_specs=[VMEM] * 6,
        out_specs=VMEM,
        compiler_params=params(24),
        name="merge_last",
    )(*finals)
    returned = lax.all_to_all(outgoing.reshape(groups, span, feature), "index", split_axis=0, concat_axis=0, tiled=True)

    logs = returned[:, capacity * share : capacity * share + 4 * PIECES].astype(F32)
    logs = jnp.sum(logs.reshape(groups, PIECES, CHUNKS, STRIDE), axis=1)
    logs = lax.dynamic_slice_in_dim(logs, (index % (groups // 2)) * sub, sub, 2).reshape(slots)
    logs = logs + travel(logs, 1) + travel(logs, -1) + travel(logs, 2)
    pair_scores = logs[place].reshape(query_count, list_len)
    highest = jnp.max(pair_scores, axis=1, keepdims=True)
    log_total = highest[:, 0] + jnp.log(jnp.sum(jnp.exp(pair_scores - highest), axis=1))
    losses = log_total - pair_scores[:, 0]
    probability = jnp.exp(pair_scores - log_total[:, None])
    target = (jnp.arange(list_len) == 0).astype(F32)
    coefficient = LOSS_SCALE * (probability - target[None, :])

    quarter = pl.pallas_call(
        functools.partial(gradient_kernel, share, list_len),
        out_shape=jax.ShapeDtypeStruct((query_count * share, feature), BF16),
        in_specs=[SMEM, SMEM, VMEM],
        out_specs=VMEM,
        scratch_shapes=[pltpu.VMEM((groups * span, feature), F32)],
        compiler_params=params(32),
        name="gradients",
    )(tile, coefficient.reshape(pairs), returned.reshape(groups * span, feature))
    gathered = lax.all_gather(quarter.reshape(query_count, share, feature), "rep")
    gradients = jnp.transpose(gathered, (1, 0, 2, 3)).reshape(query_count, query_len, feature)
    return (losses, gradients)


def solution(mesh):
    return jax.shard_map(
        per_device,
        mesh=mesh,
        in_specs=(
            P("index", None, None),
            P("index", None),
            P(),
            P("index"),
            P("index", "rep", None),
        ),
        out_specs=(P("index"), P("index", None, None)),
        check_vma=False,
    )
```

```python
import functools
import math

import jax
import jax.numpy as jnp
from jax import lax
from jax.experimental import pallas as pl
from jax.experimental.pallas import tpu as pltpu
from jax.sharding import PartitionSpec as P

TAU = 0.1
LOSS_SCALE = 32.0
NEG = -1e30
BLOCK = 4
UNROLL = 32
CHUNKS = 2
LANES = 128
STRIDE = 256
PIECES = 3
F32 = jnp.float32
BF16 = jnp.bfloat16

SMEM = pl.BlockSpec(memory_space=pltpu.SMEM)
VMEM = pl.BlockSpec(memory_space=pltpu.VMEM)
ANY = pl.BlockSpec(memory_space=pl.ANY)


def params(mib):
    return pltpu.CompilerParams(vmem_limit_bytes=mib * 1024 * 1024)


def route_kernel(capacity, page_bits, list_len, listed, page_slot, table, place, tile, used):
    slots = table.shape[0]
    pairs = listed.shape[0]
    groups = used.shape[0]
    sub = capacity // CHUNKS

    def clear(i, _):
        for k in range(16):
            table[i * 16 + k] = -1
        return 0

    lax.fori_loop(0, slots // 16, clear, 0)
    for i in range(groups):
        used[i] = 0

    def step(q, _):
        for k in range(list_len):
            i = q * list_len + k
            row = page_slot[listed[i]]
            owner = lax.shift_right_logical(row, page_bits)
            n = jnp.minimum(used[owner], capacity - 1)
            used[owner] = n + 1
            chunk = n & 1
            j = lax.shift_right_logical(n, 1)
            table[owner * capacity + chunk * sub + j] = lax.shift_left(q, page_bits) + (row & ((1 << page_bits) - 1))
            place[i] = owner * capacity + chunk * sub + j
            tile[i] = owner * (capacity + 2) + chunk * sub + j
        return 0

    lax.fori_loop(0, pairs // list_len, step, 0)


def sort_kernel(capacity, page_bits, query_count, blocks, arrived, order, count, first):
    page_base = CHUNKS * blocks * BLOCK
    total_base = page_base + CHUNKS * blocks
    slots = arrived.shape[0]
    groups = slots // capacity
    sub = capacity // CHUNKS
    pages = 1 << page_bits
    nothing = (groups // 2) * sub * 2048

    def clear(i, _):
        for k in range(16):
            order[i * 16 + k] = nothing
        return 0

    lax.fori_loop(0, CHUNKS * blocks * BLOCK // 16, clear, 0)

    def clear_blocks(i, _):
        for k in range(16):
            order[page_base + i * 16 + k] = 0
        return 0

    lax.fori_loop(0, CHUNKS * blocks // 16, clear_blocks, 0)
    for i in range(CHUNKS * pages + 1):
        count[i] = 0

    def tally(s, _):
        for chunk in range(CHUNKS):
            for j in range(sub):
                code = arrived[s * capacity + chunk * sub + j]
                p = jnp.where(code < 0, CHUNKS * pages, (code & (pages - 1)) + chunk * pages)
                count[p] = count[p] + 1
        return 0

    lax.fori_loop(0, groups, tally, 0)

    for chunk in range(CHUNKS):

        def lay(p, b):
            n = count[chunk * pages + p]
            first[chunk * pages + p] = b * BLOCK
            count[chunk * pages + p] = 0
            steps = lax.shift_right_logical(n + BLOCK - 1, 2)

            def one(k, _):
                order[page_base + b + k] = p
                return 0

            lax.fori_loop(0, steps, one, 0)
            return b + steps

        total = lax.fori_loop(0, pages, lay, jnp.int32(chunk * blocks))
        order[total_base + chunk] = total - chunk * blocks
    first[CHUNKS * pages] = total_base + 8
    count[CHUNKS * pages] = 0

    def source(s, _):
        side = lax.shift_right_logical(s, 4)
        slot = side * STRIDE + (s & 15) * sub
        base = s * query_count + slot * 2048
        for chunk in range(CHUNKS):
            for j in range(sub):
                code = arrived[s * capacity + chunk * sub + j]
                p = jnp.where(code < 0, CHUNKS * pages, (code & (pages - 1)) + chunk * pages)
                q = lax.shift_right_logical(jnp.maximum(code, 0), page_bits)
                r = count[p]
                count[p] = r + 1
                order[first[p] + r] = q + base + j * 2048
        return 0

    lax.fori_loop(0, groups, source, 0)


def split(x):
    parts = []
    for _ in range(PIECES):
        part = x.astype(BF16)
        parts.append(part)
        x = x - part.astype(F32)
    return parts


def pair_kernel(chunk, blocks, scale, order, limits, me, *refs):
    page_base = CHUNKS * blocks * BLOCK
    total_base = page_base + CHUNKS * blocks
    pages, held = refs[:2]
    outs = refs[2:10]
    wide, stats = refs[10:]
    part = pages.shape[1]
    tokens = held.shape[1]
    share = tokens // 4
    power = scale * math.log2(math.e)
    lane = lax.broadcasted_iota(jnp.int32, (1, part), 1)
    lanes = lax.broadcasted_iota(jnp.int32, (tokens, LANES), 1)

    def step(it, _):
        for u in range(UNROLL):
            b = chunk * blocks + it * UNROLL + u
            p = order[page_base + b]
            codes = [order[b * BLOCK + i] for i in range(BLOCK)]
            block = jnp.concatenate([held[c & 2047] for c in codes], axis=0)
            page = pages[p]
            raw = lax.dot_general(block, page, (((1,), (1,)), ((), ())), preferred_element_type=F32)
            raw = jnp.where(lane < limits[p], raw, NEG)
            top = jnp.max(raw, axis=1, keepdims=True)
            weights = jnp.exp2((raw - top) * power)
            total = jnp.sum(weights, axis=1, keepdims=True)
            out = jnp.dot(weights.astype(BF16), page, preferred_element_type=F32)
            peak = jnp.maximum(top * scale, NEG)
            for i in range(BLOCK):
                slot = lax.shift_right_logical(codes[i], 11)
                for t in range(4):
                    first = i * tokens + t * share
                    wide[t, pl.ds(pl.multiple_of(slot * share, share), share), :] = out[first : first + share]
                here = lanes == (slot & (LANES - 1))
                at = lax.shift_right_logical(slot, 7)
                rows = slice(i * tokens, (i + 1) * tokens)
                stats[0, at] = jnp.where(here, peak[rows], stats[0, at])
                stats[1, at] = jnp.where(here, total[rows], stats[1, at])
        return 0

    lax.fori_loop(0, (order[total_base + chunk] + UNROLL - 1) // UNROLL, step, 0)

    rep = me[0]
    length = outs[0].shape[0] - 2 * PIECES * 2 * share
    piece = 512
    for p in range(4):
        t = (rep + p) & 3
        for h in range(2):
            out = outs[p * 2 + h]

            def narrow(i, _):
                at = pl.multiple_of(i * piece, piece)
                out[pl.ds(at, piece), :] = wide[t, pl.ds(at + h * STRIDE * share, piece), :].astype(BF16)
                return 0

            lax.fori_loop(0, length // piece, narrow, 0)
            for s in range(2):
                rows = pl.ds(pl.multiple_of(t * share, share), share)
                both = jnp.concatenate([stats[s, h * 2, rows, :], stats[s, h * 2 + 1, rows, :]], axis=0)
                for k, x in enumerate(split(both)):
                    at = length + (s * PIECES + k) * 2 * share
                    out[at : at + 2 * share, :] = x


def merge_kernel(last, root, share, sub, *refs):
    n_in = 4
    ins = refs[:n_in]
    outs = refs[-1:] if last == 2 else refs[n_in:]
    length = ins[0].shape[0] - 2 * PIECES * 2 * share
    span = 2 * sub * share + 2 * share
    for n in range(n_in // 2):
        chunk, h = max(last - 1, 0), n % 2
        came, own = ins[2 * n], ins[2 * n + 1]

        def joined(ref, s):
            at = length + s * PIECES * 2 * share
            tiles = [ref[at + k * 2 * share : at + (k + 1) * 2 * share, :].astype(F32) for k in range(PIECES)]
            return tiles[0] + (tiles[1] + tiles[2])

        peak_a, total_a, peak_b, total_b = joined(came, 0), joined(came, 1), joined(own, 0), joined(own, 1)
        peak = jnp.maximum(peak_a, peak_b)
        part_a, part_b = jnp.exp(peak_a - peak), jnp.exp(peak_b - peak)
        total = total_a * part_a + total_b * part_b
        if last:
            part_a, part_b = part_a / (total * root), part_b / (total * root)
            logs = TAU * (peak + jnp.log(total))
            rows = [jnp.sum(logs[k * share : (k + 1) * share], axis=0, keepdims=True) for k in range(2)]
            if chunk == 0:
                outs[1][2 * h : 2 * h + 2, :] = jnp.concatenate(rows, axis=0)
            else:
                both = jnp.concatenate([refs[n_in + 1][2 * h : 2 * h + 2, :]] + rows, axis=0)
                tile = jnp.concatenate([x.astype(F32) for x in split(both)] + [both * 0.0], axis=0).astype(BF16)
                sources = length // (sub * share)
                for source in range(sources):
                    at = (h * sources + source) * span + 2 * sub * share
                    outs[0][at : at + 2 * share, :] = tile
        else:
            for s, x in enumerate((peak, total)):
                for k, tile in enumerate(split(x)):
                    at = length + (s * PIECES + k) * 2 * share
                    outs[h][at : at + 2 * share, :] = tile
        for pair in range(length // (2 * share)):
            at = pair * 2 * share

            def factor(x):
                columns = []
                for slot in (2 * pair, 2 * pair + 1):
                    k, lane = slot // LANES, slot % LANES
                    columns.append(jnp.broadcast_to(x[k * share : (k + 1) * share, lane : lane + 1], (share, LANES)))
                return jnp.concatenate(columns, axis=0)

            rows = slice(at, at + 2 * share)
            value = came[rows, :].astype(F32) * factor(part_a) + own[rows, :].astype(F32) * factor(part_b)
            if last == 1:
                outs[0][h * length + pair * 2 * share : h * length + (pair + 1) * 2 * share, :] = value.astype(BF16)
            elif last:
                source, j = 2 * pair // sub, 2 * pair % sub
                to = (h * (length // (sub * share)) + source) * span + (chunk * sub + j) * share
                outs[0][to : to + 2 * share, :] = value.astype(BF16)
                earlier = h * length + pair * 2 * share
                to = to - sub * share
                outs[0][to : to + 2 * share, :] = refs[n_in][earlier : earlier + 2 * share, :]
            else:
                outs[h][rows, :] = value.astype(BF16)


def gradient_kernel(share, list_len, place, weight, directions, out, wide):
    def widen(i, _):
        at = pl.multiple_of(i * 128, 128)
        wide[pl.ds(at, 128), :] = directions[pl.ds(at, 128), :].astype(F32)
        return 0

    lax.fori_loop(0, directions.shape[0] // 128, widen, 0)

    def step(i, _):
        parts = []
        for s in range(2):
            total = jnp.zeros((share, out.shape[1]), F32)
            for k in range(list_len):
                e = (i * 2 + s) * list_len + k
                at = pl.multiple_of(place[e] * share, share)
                total = total + weight[e] * wide[pl.ds(at, share), :]
            parts.append(total)
        out[pl.ds(pl.multiple_of(i * 2 * share, 2 * share), 2 * share), :] = jnp.concatenate(parts, axis=0).astype(BF16)
        return 0

    lax.fori_loop(0, out.shape[0] // share // 2, step, 0)


def ints(*shape):
    return jax.ShapeDtypeStruct(shape, jnp.int32)


def per_device(queries, listed, page_slot, counts, page_store):
    groups = lax.axis_size("index")
    index = lax.axis_index("index").astype(jnp.int32)
    rep = lax.axis_index("rep").astype(jnp.int32)
    reps = lax.axis_size("rep")
    query_count, query_len, feature = queries.shape
    list_len = listed.shape[1]
    pages, part, _ = page_store.shape
    page_bits = pages.bit_length() - 1
    pairs = query_count * list_len
    capacity = 2 * pairs // groups
    sub = capacity // CHUNKS
    slots = groups * capacity
    share = query_len // reps
    blocks = (groups * sub + (BLOCK - 1) * pages) // BLOCK
    blocks = (blocks + UNROLL - 1) // UNROLL * UNROLL
    root = math.sqrt(feature)
    scale = 1.0 / (root * TAU)

    table, place, tile = pl.pallas_call(
        functools.partial(route_kernel, capacity, page_bits, list_len),
        out_shape=(ints(slots), ints(pairs), ints(pairs)),
        in_specs=[SMEM, SMEM],
        out_specs=(SMEM,) * 3,
        scratch_shapes=[pltpu.SMEM((groups,), jnp.int32)],
        name="route",
    )(listed.reshape(pairs), page_slot)
    arrived = lax.all_to_all(table.reshape(groups, capacity), "index", split_axis=0, concat_axis=0, tiled=True)

    everyone = lax.all_gather(queries, "index", tiled=True)

    order = pl.pallas_call(
        functools.partial(sort_kernel, capacity, page_bits, query_count, blocks),
        out_shape=ints(CHUNKS * blocks * (BLOCK + 1) + 8 + slots),
        in_specs=[SMEM],
        out_specs=SMEM,
        scratch_shapes=[pltpu.SMEM((CHUNKS * pages + 1,), jnp.int32)] * 2,
        cost_estimate=pl.CostEstimate(flops=0, bytes_accessed=40_000_000, transcendentals=0),
        name="sort_pairs",
    )(arrived.reshape(slots))

    limits = counts - rep * part
    me = rep[None]

    length = groups // 2 * sub * share
    packed = length + 2 * PIECES * 2 * share

    def rep_pairs(step):
        return [(i, (i + step) % reps) for i in range(reps)]

    def travel(x, step):
        return lax.ppermute(x, "rep", rep_pairs(step))

    finals = []
    for chunk in range(CHUNKS):
        parts = pl.pallas_call(
            functools.partial(pair_kernel, chunk, blocks, scale),
            out_shape=(jax.ShapeDtypeStruct((packed, feature), BF16),) * 8,
            in_specs=[SMEM] * 3 + [VMEM] * 2,
            out_specs=(VMEM,) * 8,
            scratch_shapes=[
                pltpu.VMEM((4, 2 * STRIDE * share, feature), F32),
                pltpu.VMEM((2, 2 * STRIDE // LANES, query_len, LANES), F32),
            ],
            compiler_params=params(28),
            cost_estimate=pl.CostEstimate(flops=0, bytes_accessed=60_000_000, transcendentals=0),
            name="pairs",
        )(order, limits, me, page_store, everyone)

        held = [parts[3 * 2], parts[1 * 2 + 1]]
        for hop in range(3):
            came = [travel(held[0], 1), travel(held[1], -1)]
            own = [parts[(2, 1, 0)[hop] * 2], parts[(2, 3, 0)[hop] * 2 + 1]]
            if hop == 2:
                finals = [came[0], own[0], came[1], own[1], *finals]
                if chunk == 0:
                    finals = pl.pallas_call(
                        functools.partial(merge_kernel, 1, root, share, sub),
                        out_shape=(jax.ShapeDtypeStruct((2 * length, feature), BF16), jax.ShapeDtypeStruct((4, LANES), F32)),
                        in_specs=[VMEM] * 4,
                        out_specs=(VMEM,) * 2,
                        compiler_params=params(24),
                        cost_estimate=pl.CostEstimate(flops=0, bytes_accessed=8_000_000, transcendentals=0),
                        name="merge_first",
                    )(*finals)
                break
            held = pl.pallas_call(
                functools.partial(merge_kernel, 0, root, share, sub),
                out_shape=(jax.ShapeDtypeStruct((packed, feature), BF16),) * 2,
                in_specs=[VMEM] * 4,
                out_specs=(VMEM,) * 2,
                compiler_params=params(24),
                cost_estimate=pl.CostEstimate(flops=0, bytes_accessed=8_000_000, transcendentals=0),
                name="merge",
            )(came[0], own[0], came[1], own[1])
    span = 2 * sub * share + 2 * share
    outgoing = pl.pallas_call(
        functools.partial(merge_kernel, 2, root, share, sub),
        out_shape=jax.ShapeDtypeStruct((groups * span, feature), BF16),
        in_specs=[VMEM] * 6,
        out_specs=VMEM,
        compiler_params=params(24),
        name="merge_last",
    )(*finals)
    returned = lax.all_to_all(outgoing.reshape(groups, span, feature), "index", split_axis=0, concat_axis=0, tiled=True)

    logs = returned[:, capacity * share : capacity * share + 4 * PIECES].astype(F32)
    logs = jnp.sum(logs.reshape(groups, PIECES, CHUNKS, STRIDE), axis=1)
    logs = lax.dynamic_slice_in_dim(logs, (index % (groups // 2)) * sub, sub, 2).reshape(slots)
    logs = logs + travel(logs, 1) + travel(logs, -1) + travel(logs, 2)
    pair_scores = logs[place].reshape(query_count, list_len)
    highest = jnp.max(pair_scores, axis=1, keepdims=True)
    log_total = highest[:, 0] + jnp.log(jnp.sum(jnp.exp(pair_scores - highest), axis=1))
    losses = log_total - pair_scores[:, 0]
    probability = jnp.exp(pair_scores - log_total[:, None])
    target = (jnp.arange(list_len) == 0).astype(F32)
    coefficient = LOSS_SCALE * (probability - target[None, :])

    quarter = pl.pallas_call(
        functools.partial(gradient_kernel, share, list_len),
        out_shape=jax.ShapeDtypeStruct((query_count * share, feature), BF16),
        in_specs=[SMEM, SMEM, VMEM],
        out_specs=VMEM,
        scratch_shapes=[pltpu.VMEM((groups * span, feature), F32)],
        compiler_params=params(32),
        name="gradients",
    )(tile, coefficient.reshape(pairs), returned.reshape(groups * span, feature))
    gathered = lax.all_gather(quarter.reshape(query_count, share, feature), "rep")
    gradients = jnp.transpose(gathered, (1, 0, 2, 3)).reshape(query_count, query_len, feature)
    return (losses, gradients)


def solution(mesh):
    return jax.shard_map(
        per_device,
        mesh=mesh,
        in_specs=(
            P("index", None, None),
            P("index", None),
            P(),
            P("index"),
            P("index", "rep", None),
        ),
        out_specs=(P("index"), P("index", None, None)),
        check_vma=False,
    )
```
